128 devices in a mesh: flow: 8 (over x, core), cross: 16 (over y, z).
Axes of the slice: x: 4, y: 4, z: 4, core: 2. Of those that a mesh axis runs over, the one named last changes fastest.
Arguments:
- matrix_start: float32 [32, 128, 512], P('flow', 'cross'), may hold values from -6 to 6
- storage: float32 [32, 128, 512], P('flow', 'cross'), may hold values from 0.1 to 1
- perm: float32 [32, 128, 512], P('flow', 'cross'), may hold values from 0.3 to 3
- frac_start: float32 [3072, 256], P(('flow', 'cross')), may hold values from -6 to 6
- frac_store: float32 [3072, 256], P(('flow', 'cross')), may hold values from 0.05 to 0.5
- frac_cond: float32 [3072, 256], P(('flow', 'cross')), may hold values from 2 to 20
- segment_ids: int32 [3072, 256], P(('flow', 'cross')), may hold values from 0 to 7, never falling along the last dimension, each value on 1 to 64 neighbouring positions
- block_counts: int32 [128], P(('flow', 'cross')), may hold values from 1 to 24, 1024 in all
- hit_tile: int32 [3072, 256, 1], P(('flow', 'cross')), may hold values from 0 to 127; in each aligned block of 6144 rows (0 to 6143, 6144 to 12287, ..., all dimensions but the last counted through in order) at most 72 rows name the same one
- hit_cell: int32 [3072, 256], P(('flow', 'cross')), may hold values from 0 to 16383
- hit_weight: float32 [3072, 256], P(('flow', 'cross')), may hold values from 1 to 8
Outputs:
- matrix_pressure: float32 [32, 128, 512], P('flow', 'cross')
- frac_pressure: float32 [3072, 256], P(('flow', 'cross'))
The draws below stay inside these ranges and needn't reach their ends.
Inputs may be any that keep to these rules, and one draw needn't show every extreme that they name: `hit_tile`: in the 6144 rows of one owner, at most 72 fracture cells lie in one matrix tile, and in some owners exactly 72 do. Tile t is the one with flow index t // 16 and cross index t % 16. `block_counts`: the counts sum to 1024 and the largest is exactly 24. `segment_ids`: within a block the ids never fall, and each segment holds 1 to 64 cells.
All inputs are finite; a program needn't handle non-finite values.
Results may differ from the reference program's by a relative error of at most 0.0001.
Values sent between devices are 32-bit elements; how exact they have to be, the bound alone decides.
No kernel may reach another device: no remote copies, remote signals or barrier semaphores. Data moves between devices by JAX's collectives and lax.ppermute only.
A program may use at most 64 MiB of HBM per device.

```python
import math
import jax
import jax.numpy as jnp
import numpy as np

CX = 4
CY = 8
CZ = 512
BLK_DEV = 24
FB = 256
SWEEPS = 4
NX = 32
NY = 128
NZ = 512
BLOCKS = 3072
CAP = 72
N_CROSS = 16
DEVICES = 128


def plant(values, stream_key, least, largest):
    longest = values.shape.index(max(values.shape))
    spots = []
    for shift in (0, 1):
        where = [jax.random.randint(jax.random.fold_in(stream_key, axis), (), 0, length) for axis, length in enumerate(values.shape)]
        where[longest] = (where[longest] + shift) % values.shape[longest]
        spots.append(tuple(where))
    return values.at[spots[0]].set(least).at[spots[1]].set(largest)


def level_of(own_key, extent, cuts, least, high):
    loudness = 1.0
    for dim, shards_of in cuts:
        heights = jax.random.uniform(jax.random.fold_in(jax.random.fold_in(own_key, 6), dim), (shards_of,), jnp.float32, least / len(cuts), high / len(cuts))
        loudness = loudness * jnp.repeat(jnp.exp(heights), extent[dim] // shards_of).reshape((-1,) + (1,) * (len(extent) - 1 - dim))
    return loudness


def split_up(count, total, most, skew):
    weights = [(1 << 20) // math.isqrt(standing ** skew) + 1 for standing in range(2, count + 1)]
    rest, counts = total - most - (count - 1), [1] * (count - 1)
    while rest > 0:
        candidates = [i for i in range(count - 1) if counts[i] < most]
        whole, budget = sum([weights[i] for i in candidates]), rest
        for i in candidates:
            addition = min(most - counts[i], max(1, budget * weights[i] // whole), rest)
            counts[i] = counts[i] + addition
            rest = rest - addition
    return np.array([most] + counts)


def ragged(own_key, number_of, total, limit, slope):
    if number_of == 2:
        one = jax.random.randint(own_key, (), max(1, total - limit), min(limit, total - 1) + 1)
        return jnp.stack([one, total - one])
    sizes = jnp.asarray(split_up(number_of, total, limit, slope), jnp.int32)
    couples = (number_of - 1) // 2
    donor, sink = sizes[1:1 + 2 * couples:2], sizes[2:2 + 2 * couples:2]
    margin = jnp.minimum(donor - 1, limit - sink)
    moved = jax.random.randint(jax.random.fold_in(own_key, 1), (couples,), 0, 1 << 20) % (margin + 1)
    sizes = sizes.at[1:1 + 2 * couples:2].set(donor - moved).at[2:2 + 2 * couples:2].set(sink + moved)
    return sizes[jax.random.permutation(jax.random.fold_in(own_key, 2), number_of)]


def deal_out(stream_key, own, number, rows, amount, top, reach, skew):
    ranking = jax.random.permutation(stream_key, amount)
    heavy_load, common = load_shares(amount, rows * top, reach, skew, True), load_shares(amount, rows * top, reach, skew, False)
    places = jnp.arange(amount)

    def named(lengths, turn):
        used = int((lengths > 0).sum())
        fixed = max(1, used // 4)
        passed = fixed + (places - fixed + turn * (used - fixed)) % max(1, amount - fixed)
        return jnp.zeros((amount,), jnp.int32).at[ranking[jnp.where(places < fixed, places, passed)]].set(jnp.asarray(lengths, jnp.int32))

    lengths = jnp.where(number % 4 == 0, named(heavy_load, number // 4), named(common, number - number // 4 - 1))
    mixed = jax.random.permutation(jax.random.fold_in(own, 3), amount)
    source_of, receiver = mixed[0:amount // 2 * 2:2], mixed[1:amount // 2 * 2:2]
    room = jnp.minimum(lengths[source_of] - 1, reach - lengths[receiver]) // 2
    room = jnp.where((source_of == ranking[0]) | (receiver == ranking[0]) | (lengths[receiver] == 0), 0, jnp.maximum(room, 0))
    passed = jax.random.randint(jax.random.fold_in(own, 4), (amount // 2,), 0, 1 << 20) % (room + 1)
    lengths = lengths.at[source_of].add(-passed).at[receiver].add(passed)
    labels = jnp.searchsorted(jnp.cumsum(lengths), jnp.arange(rows * top), side="right").astype(jnp.int32)
    listing = labels.reshape(top, rows).T
    listing = listing[jax.random.permutation(jax.random.fold_in(own, 1), rows)]
    turn = jax.random.randint(jax.random.fold_in(own, 2), (rows, 1), 0, top)
    return jnp.take_along_axis(listing, (jnp.arange(top)[None, :] + turn) % top, axis=1)


def load_shares(amount, total, most, skew, full):
    portions = [(1 << 20) // math.isqrt(standing ** skew) + 1 for standing in range(1, amount + 1)]
    largest = most if full else min(most, max(-(-total // amount), total * portions[0] // sum(portions)))
    least = 1 if total - largest >= amount - 1 else 0
    given, spare = [largest] + [least] * (amount - 1), total - largest - least * (amount - 1)
    while spare > 0:
        candidates = [i for i in range(1, amount) if given[i] < largest] or [i for i in range(1, amount) if given[i] < most]
        whole, remaining = sum([portions[i] for i in candidates]), spare
        for i in candidates:
            extra = min(most - given[i], max(1, remaining * portions[i] // whole), spare)
            given[i] = given[i] + extra
            spare = spare - extra
    return np.array(given)


def noise(own_key, extent, scale, most, cuts=(), kind=jnp.bfloat16):
    result = jax.random.normal(own_key, extent, jnp.float32) * scale
    if len(cuts) > 0:
        result = level_of(own_key, extent, cuts, -0.22, 0.18) * result
    return jnp.clip(result, min=-most, max=most).astype(kind)


def setup_inputs(seed: int = 0) -> dict:
    arg_keys = jax.random.split(jax.random.key(seed), 12)
    matrix_start = noise(arg_keys[0], (NX, NY, NZ), 1.0, 6.0, ((0, 8), (1, 16)), jnp.float32)
    storage = jnp.clip(jnp.exp(math.log(1.0) - 2.3025851 * jax.random.uniform(arg_keys[1], (NX, NY, NZ), jnp.float32) ** level_of(arg_keys[1], (NX, NY, NZ), ((0, 8), (1, 16)), -0.2, 0.2)), 0.1, 1.0)
    perm = jnp.clip(jnp.exp(math.log(3.0) - 2.3025851 * jax.random.uniform(arg_keys[2], (NX, NY, NZ), jnp.float32) ** level_of(arg_keys[2], (NX, NY, NZ), ((0, 8), (1, 16)), -0.2, 0.2)), 0.3, 3.0)
    frac_start = noise(arg_keys[3], (BLOCKS, FB), 1.0, 6.0, ((0, 128),), jnp.float32)
    frac_store = jnp.clip(jnp.exp(math.log(0.5) - 2.3025851 * jax.random.uniform(arg_keys[4], (BLOCKS, FB), jnp.float32) ** level_of(arg_keys[4], (BLOCKS, FB), ((0, 128),), -0.2, 0.2)), 0.05, 0.5)
    frac_cond = jnp.clip(jnp.exp(math.log(20.0) - 2.3025851 * jax.random.uniform(arg_keys[5], (BLOCKS, FB), jnp.float32) ** level_of(arg_keys[5], (BLOCKS, FB), ((0, 128),), -0.2, 0.2)), 2.0, 20.0)
    segment_ids = jax.vmap(lambda own: jnp.searchsorted(jnp.cumsum(ragged(own, 8, FB, 64, 1)), jnp.arange(FB), side="right"))(jax.random.split(arg_keys[6], BLOCKS)).reshape((BLOCKS, FB)).astype(jnp.int32)
    block_counts = ragged(arg_keys[7], DEVICES, BLOCKS // 3, BLK_DEV, 2).astype(jnp.int32)
    hit_tile_keys = jax.random.split(jax.random.fold_in(arg_keys[8], 1), BLOCKS * FB // (BLK_DEV * FB))
    hit_tile_turns = jax.random.permutation(jax.random.fold_in(arg_keys[8], 3), BLOCKS * FB // (BLK_DEV * FB))
    hit_tile = jax.vmap(lambda own, number: deal_out(jax.random.fold_in(arg_keys[8], 2), own, number, BLK_DEV * FB, DEVICES, 1, CAP, 1))(hit_tile_keys, hit_tile_turns).reshape((BLOCKS, FB, 1))
    hit_cell = plant(jax.random.randint(arg_keys[9], (BLOCKS, FB), 0, CX * CY * CZ), jax.random.fold_in(arg_keys[9], 1), 0, (CX * CY * CZ) - 1).astype(jnp.int32)
    hit_weight = jnp.clip(jnp.exp(math.log(8.0) - 2.0794415 * jax.random.uniform(arg_keys[10], (BLOCKS, FB), jnp.float32) ** level_of(arg_keys[10], (BLOCKS, FB), ((0, 128),), -0.2, 0.2)), 1.0, 8.0)
    return dict(matrix_start=matrix_start, storage=storage, perm=perm, frac_start=frac_start, frac_store=frac_store, frac_cond=frac_cond, segment_ids=segment_ids, block_counts=block_counts, hit_tile=hit_tile, hit_cell=hit_cell, hit_weight=hit_weight)


def beside(padded):
    return [padded[:-2, 1:-1, 1:-1], padded[2:, 1:-1, 1:-1], padded[1:-1, :-2, 1:-1],
            padded[1:-1, 2:, 1:-1], padded[1:-1, 1:-1, :-2], padded[1:-1, 1:-1, 2:]]


def transmit(centre, neighbours):
    return [2.0 * centre * neighbour / (centre + neighbour) for neighbour in neighbours]


def chain_links(frac_cond, segment_ids):
    linked = (segment_ids[:, :-1] == segment_ids[:, 1:]).astype(jnp.float32)
    zero_col = jnp.zeros_like(frac_cond[:, :1])
    link_right = jnp.concatenate([frac_cond[:, :-1] * linked, zero_col], axis=1)
    link_left = jnp.concatenate([zero_col, link_right[:, :-1]], axis=1)
    return link_left, link_right


def fracture_update(frac_now, frac_start, frac_store, link_left, link_right, weight_live, matrix_seen, live_mask):
    zero_col = jnp.zeros_like(frac_now[:, :1])
    left_value = jnp.concatenate([zero_col, frac_now[:, :-1]], axis=1)
    right_value = jnp.concatenate([frac_now[:, 1:], zero_col], axis=1)
    numerator = frac_store * frac_start + link_left * left_value + link_right * right_value + weight_live * matrix_seen
    denominator = frac_store + link_left + link_right + weight_live
    return jnp.where(live_mask, numerator / denominator, frac_start)


def reference(matrix_start, storage, perm, frac_start, frac_store, frac_cond, segment_ids, block_counts, hit_tile, hit_cell, hit_weight):
    conduct = transmit(perm, beside(jnp.pad(perm, 1)))
    cond_total = sum(conduct)
    block_index = jnp.arange(BLOCKS, dtype=jnp.int32)
    live_mask = ((block_index % BLK_DEV) < block_counts[block_index // BLK_DEV])[:, None]
    weight_live = jnp.where(live_mask, hit_weight, jnp.zeros_like(hit_weight))
    tile_id = hit_tile[:, :, 0]
    glob_x = (tile_id // N_CROSS) * CX + hit_cell // (CY * CZ)
    glob_y = (tile_id % N_CROSS) * CY + (hit_cell // CZ) % CY
    glob_z = hit_cell % CZ
    flat_cell = ((glob_x * NY + glob_y) * NZ + glob_z).reshape(-1).astype(jnp.int32)
    total_cells = NX * NY * NZ
    weight_sum = jnp.zeros((total_cells,), jnp.float32).at[flat_cell].add(weight_live.reshape(-1)).reshape(NX, NY, NZ)
    matrix_denom = storage + cond_total + weight_sum
    matrix_source = storage * matrix_start
    link_left, link_right = chain_links(frac_cond, segment_ids)
    matrix_now, frac_now = matrix_start, frac_start
    for sweep_no in range(SWEEPS):
        views = beside(jnp.pad(matrix_now, 1))
        inflow = sum(face * view for face, view in zip(conduct, views))
        transfer = jnp.zeros((total_cells,), jnp.float32).at[flat_cell].add((weight_live * frac_now).reshape(-1)).reshape(NX, NY, NZ)
        matrix_seen = matrix_now.reshape(-1)[flat_cell].reshape(BLOCKS, FB)
        matrix_next = (matrix_source + inflow + transfer) / matrix_denom
        frac_now = fracture_update(frac_now, frac_start, frac_store, link_left, link_right, weight_live, matrix_seen, live_mask)
        matrix_now = matrix_next
    return matrix_now, frac_now
```

```python
import functools

import jax
import jax.numpy as jnp
from jax import lax
from jax.experimental import pallas as pl
from jax.experimental.pallas import tpu as pltpu
from jax.sharding import PartitionSpec as P

F32 = jnp.float32
BF16 = jnp.bfloat16
I32 = jnp.int32

LANES = 256
HALF_RANKS = 36
PAD_RANKS = 40
ROWS = 64
VMEM_LIMIT = 48 * 1024 * 1024

NN = (((1,), (0,)), ((), ()))
NT = (((1,), (1,)), ((), ()))


def call(body, out_shape, n_in, scratch=(), smem=(), cost=1000000):
    in_specs = [
        pl.BlockSpec(memory_space=pltpu.SMEM if i in smem else pltpu.VMEM) for i in range(n_in)
    ]
    out_specs = jax.tree.map(lambda _: pl.BlockSpec(memory_space=pltpu.VMEM), out_shape)
    return pl.pallas_call(
        body,
        out_shape=out_shape,
        in_specs=in_specs,
        out_specs=out_specs,
        scratch_shapes=list(scratch),
        compiler_params=pltpu.CompilerParams(vmem_limit_bytes=VMEM_LIMIT),
        cost_estimate=pl.CostEstimate(flops=cost, bytes_accessed=cost, transcendentals=0),
    )


def shape(*dims, dtype=F32):
    return jax.ShapeDtypeStruct(dims, dtype)


def halves(value):
    high = value.astype(BF16)
    low = (value - high.astype(F32)).astype(BF16)
    return high, low


def one_hot(index_row, count):
    place = lax.broadcasted_iota(I32, (count, LANES), 0)
    return place == index_row


def as_bf16(mask):
    return jnp.where(mask, 1.0, 0.0).astype(BF16)


def shift_right(x):
    return pltpu.roll(x, 1, 1)


def shift_left(x):
    return pltpu.roll(x, LANES - 1, 1)


def store_slots(out_ref, by_slot, group, groups):
    rows = by_slot.shape[0]
    if rows < 128:
        by_slot = jnp.concatenate([by_slot, jnp.zeros((128 - rows, LANES), F32)], axis=0)
    turned = by_slot.T
    for part in range(2):
        out_ref[pl.ds(group * 2 + part, 128, stride=2 * groups), :] = turned[
            part * 128 : part * 128 + 128
        ]


def load_slots(in_ref, group, groups):
    parts = [in_ref[pl.ds(group * 2 + part, 128, stride=2 * groups), :] for part in range(2)]
    return jnp.concatenate(parts, axis=0).T


def owner_first(
    count_ref,
    start_ref,
    store_ref,
    cond_ref,
    seg_ref,
    tile_ref,
    cell_ref,
    weight_ref,
    out_ref,
    coef_ref,
    slot_ref,
    key_hot,
    spread,
    values,
):
    blocks = start_ref.shape[0]
    size = (blocks, LANES)
    live = lax.broadcasted_iota(I32, size, 0) < count_ref[0]
    lane = lax.broadcasted_iota(I32, size, 1)
    start = start_ref[...]
    store = store_ref[...]
    weight = jnp.where(live, weight_ref[...], 0.0)
    seg = seg_ref[...]
    linked = (seg == shift_left(seg)) & (lane < LANES - 1)
    right = jnp.where(linked, cond_ref[...], 0.0)
    left = shift_right(right)
    inverse = 1.0 / (store + left + right + weight)
    own = jnp.where(live, store * start * inverse, start)
    left = jnp.where(live, left * inverse, 0.0)
    right = jnp.where(live, right * inverse, 0.0)
    pull = weight * inverse
    coef_ref[0] = own
    coef_ref[1] = left
    coef_ref[2] = right
    coef_ref[3] = pull
    coef_ref[4] = weight
    partial = own + left * shift_right(start) + right * shift_left(start)
    values[0] = cell_ref[...].astype(F32)
    values[1] = weight
    values[2] = weight * start
    values[3] = weight * partial
    values[4] = weight * pull
    slot_ref[0] = jnp.where(live, tile_ref[...], -1)
    upper = as_bf16(
        lax.broadcasted_iota(I32, (LANES, LANES), 0) <= lax.broadcasted_iota(I32, (LANES, LANES), 1)
    )

    def step(b, seen_before):
        target = slot_ref[0, pl.ds(b, 1), :]
        hot = one_hot(target, 128)
        running = lax.dot_general(as_bf16(hot), upper, NN, preferred_element_type=F32) + seen_before
        rank = jnp.sum(jnp.where(hot, running, 0.0), axis=0, keepdims=True).astype(I32) - 1
        rank = jnp.maximum(rank, 0)
        key = jnp.where(target >= 0, target + (rank & 1) * 128, -1)
        rank_half = rank >> 1
        slot_ref[0, pl.ds(b, 1), :] = key
        slot_ref[1, pl.ds(b, 1), :] = rank_half
        key_hot[b] = as_bf16(one_hot(key, LANES))
        rank_hot = one_hot(rank_half, PAD_RANKS)
        rows = []
        for v in range(5):
            high, low = halves(values[v, pl.ds(b, 1), :])
            rows += [high.astype(F32), low.astype(F32)]
        spread[b] = jnp.concatenate(
            [jnp.where(rank_hot, row, 0.0) for row in rows], axis=0
        ).astype(BF16)
        return running[:, LANES - 1 :]

    lax.fori_loop(0, blocks, step, jnp.zeros((128, 1), F32))
    total = jnp.zeros((10 * PAD_RANKS, LANES), F32)
    for b in range(blocks):
        total += lax.dot_general(spread[b], key_hot[b], NT, preferred_element_type=F32)
    sums = [
        total[2 * v * PAD_RANKS : (2 * v + 1) * PAD_RANKS]
        + total[(2 * v + 1) * PAD_RANKS : (2 * v + 2) * PAD_RANKS]
        for v in range(5)
    ]
    store_slots(out_ref, jnp.concatenate(sums[:3], axis=0), 0, 2)
    store_slots(out_ref, jnp.concatenate(sums[3:], axis=0), 1, 2)


def unpack(recv_ref, slot_ref, key_hot, seen, blocks):
    turned = load_slots(recv_ref, 0, 1)
    turned = turned[: 2 * PAD_RANKS]
    high, low = halves(turned)
    table = jnp.concatenate([high.astype(F32), low.astype(F32)], axis=0).astype(BF16)

    def step(b, carry):
        hot = as_bf16(one_hot(slot_ref[0, pl.ds(b, 1), :], LANES))
        if key_hot is not None:
            key_hot[b] = hot
        found = lax.dot_general(table, hot, NN, preferred_element_type=F32)
        found = found[: 2 * PAD_RANKS] + found[2 * PAD_RANKS :]
        rank_hot = one_hot(slot_ref[1, pl.ds(b, 1), :], PAD_RANKS)
        for v in range(2):
            mine = jnp.where(rank_hot, found[v * PAD_RANKS : (v + 1) * PAD_RANKS], 0.0)
            seen[v, pl.ds(b, 1), :] = jnp.sum(mine, axis=0, keepdims=True)
        return carry

    lax.fori_loop(0, blocks, step, 0)


def owner_middle(
    recv_ref, start_ref, coef_ref, slot_ref, out_ref, partial_ref, key_hot, spread, seen, values
):
    blocks = start_ref.shape[0]
    unpack(recv_ref, slot_ref, key_hot, seen, blocks)
    own, left, right, pull, weight = [coef_ref[i] for i in range(5)]
    now = start_ref[...]
    for v in range(2):
        now = own + left * shift_right(now) + right * shift_left(now) + pull * seen[v]
    partial = own + left * shift_right(now) + right * shift_left(now)
    partial_ref[...] = partial
    values[0] = weight * now
    values[1] = weight * partial

    def step(b, carry):
        rank_hot = one_hot(slot_ref[1, pl.ds(b, 1), :], PAD_RANKS)
        rows = []
        for v in range(2):
            high, low = halves(values[v, pl.ds(b, 1), :])
            rows += [high.astype(F32), low.astype(F32)]
        spread[b] = jnp.concatenate(
            [jnp.where(rank_hot, row, 0.0) for row in rows], axis=0
        ).astype(BF16)
        return carry

    lax.fori_loop(0, blocks, step, 0)
    total = jnp.zeros((4 * PAD_RANKS, LANES), F32)
    for b in range(blocks):
        total += lax.dot_general(spread[b], key_hot[b], NT, preferred_element_type=F32)
    sums = [
        total[2 * v * PAD_RANKS : (2 * v + 1) * PAD_RANKS]
        + total[(2 * v + 1) * PAD_RANKS : (2 * v + 2) * PAD_RANKS]
        for v in range(2)
    ]
    store_slots(out_ref, jnp.concatenate(sums, axis=0), 0, 1)


def owner_last(recv_ref, coef_ref, slot_ref, partial_ref, out_ref, seen):
    blocks = partial_ref.shape[0]
    unpack(recv_ref, slot_ref, None, seen, blocks)
    own, left, right, pull = [coef_ref[i] for i in range(4)]
    now = partial_ref[...] + pull * seen[0]
    out_ref[...] = own + left * shift_right(now) + right * shift_left(now) + pull * seen[1]


def fold(field):
    return jnp.concatenate([field[:, :LANES], field[:, LANES:]], axis=0)


def unfold(rows):
    half = ROWS // 2
    return jnp.concatenate([rows[:half], rows[half:]], axis=1)


def gather_cells(fields, cell_ref, cell_hot, found_ref):
    parts = []
    for field in fields:
        high, low = halves(fold(field))
        parts += [high, low]
    table = jnp.concatenate([p.astype(F32) for p in parts], axis=0).astype(BF16)

    def step(r, carry):
        row_hot = one_hot(cell_ref[0, pl.ds(r, 1), :], ROWS)
        found = lax.dot_general(table, cell_hot[r], NN, preferred_element_type=F32)
        for v in range(len(fields)):
            both = found[2 * v * ROWS : (2 * v + 1) * ROWS] + found[(2 * v + 1) * ROWS : (2 * v + 2) * ROWS]
            found_ref[pl.ds(v * PAD_RANKS + r, 1), :] = jnp.sum(
                jnp.where(row_hot, both, 0.0), axis=0, keepdims=True
            )
        return carry

    lax.fori_loop(0, HALF_RANKS, step, 0)


def scatter_cells(values_ref, count, cell_ref, cell_hot, spread):
    def step(r, carry):
        row_hot = one_hot(cell_ref[0, pl.ds(r, 1), :], ROWS)
        cell_hot[r] = as_bf16(one_hot(cell_ref[1, pl.ds(r, 1), :], LANES))
        rows = []
        for v in range(count):
            high, low = halves(values_ref[v, pl.ds(r, 1), :])
            rows += [high.astype(F32), low.astype(F32)]
        spread[r] = jnp.concatenate(
            [jnp.where(row_hot, row, 0.0) for row in rows], axis=0
        ).astype(BF16)
        return carry

    lax.fori_loop(0, HALF_RANKS, step, 0)
    total = jnp.zeros((2 * count * ROWS, LANES), F32)
    for r in range(HALF_RANKS):
        total += lax.dot_general(spread[r], cell_hot[r], NT, preferred_element_type=F32)
    return [
        unfold(total[2 * v * ROWS : (2 * v + 1) * ROWS] + total[(2 * v + 1) * ROWS : (2 * v + 2) * ROWS])
        for v in range(count)
    ]


def neighbours(field, x_low, x_high, y_low, y_high, ny):
    rows, nz = field.shape
    nx = rows // ny
    west = jnp.concatenate([x_low, field[: rows - ny]], axis=0)
    east = jnp.concatenate([field[ny:], x_high], axis=0)
    place = lax.broadcasted_iota(I32, (rows, nz), 0) % ny
    wide_low = jnp.concatenate(
        [jnp.broadcast_to(y_low[i : i + 1], (ny, nz)) for i in range(nx)], axis=0
    )
    wide_high = jnp.concatenate(
        [jnp.broadcast_to(y_high[i : i + 1], (ny, nz)) for i in range(nx)], axis=0
    )
    south = jnp.where(place == 0, wide_low, pltpu.roll(field, 1, 0))
    north = jnp.where(place == ny - 1, wide_high, pltpu.roll(field, rows - 1, 0))
    below = pltpu.roll(field, 1, 1)
    above = pltpu.roll(field, nz - 1, 1)
    return west, east, south, north, below, above


def rock(edge_ref, perm_ref, start_ref, storage_ref, xl, xh, yl, yh, faces_ref, base_ref):
    rows, nz = perm_ref.shape
    ny = 8
    perm = perm_ref[...]
    start = start_ref[...]
    beside = neighbours(perm, xl[0], xh[0], yl[0], yh[0], ny)
    values = neighbours(start, xl[1], xh[1], yl[1], yh[1], ny)
    row = lax.broadcasted_iota(I32, (rows, nz), 0)
    lane = lax.broadcasted_iota(I32, (rows, nz), 1)
    closed = [
        (row < ny) & (edge_ref[0] == 0),
        (row >= rows - ny) & (edge_ref[1] == 0),
        (row % ny == 0) & (edge_ref[2] == 0),
        (row % ny == ny - 1) & (edge_ref[3] == 0),
        lane == 0,
        lane == nz - 1,
    ]
    storage = storage_ref[...]
    base = storage * start
    inflow = jnp.zeros_like(start)
    total = storage
    for i in range(6):
        face = jnp.where(closed[i], 0.0, 2.0 * perm * beside[i] / (perm + beside[i]))
        faces_ref[i] = face
        total += face
        inflow += face * values[i]
    base_ref[0] = total
    base_ref[1] = base
    base_ref[2] = base + inflow


def tile_first(recv_ref, start_ref, base_ref, out_ref, next_ref, sums_ref, cells_ref,
               cell_hot, spread, values, found):
    first = load_slots(recv_ref, 0, 2)
    second = load_slots(recv_ref, 1, 2)
    cell = first[:PAD_RANKS].astype(I32)
    deep = cell & 511
    cells_ref[0] = ((deep >> 8) << 5) + (cell >> 9)
    cells_ref[1] = deep & (LANES - 1)
    values[0] = first[PAD_RANKS : 2 * PAD_RANKS]
    values[1] = first[2 * PAD_RANKS : 3 * PAD_RANKS]
    values[2] = second[:PAD_RANKS]
    values[3] = second[PAD_RANKS : 2 * PAD_RANKS]
    weight, pushed, partial, pull = scatter_cells(values, 4, cells_ref, cell_hot, spread)
    start = start_ref[...]
    inverse = 1.0 / (base_ref[0] + weight)
    now = (base_ref[2] + pushed) * inverse
    next_ref[...] = now
    sums_ref[0] = inverse
    sums_ref[1] = base_ref[1] + partial + start * pull
    sums_ref[2] = pull
    found[...] = jnp.zeros_like(found)
    gather_cells([start, now], cells_ref, cell_hot, found)
    store_slots(out_ref, found[...], 0, 1)


def flow_in(field, faces_ref, xl, xh, yl, yh):
    around = neighbours(field, xl[...], xh[...], yl[...], yh[...], 8)
    total = faces_ref[0] * around[0]
    for i in range(1, 6):
        total += faces_ref[i] * around[i]
    return total


def tile_second(now_ref, sums_ref, faces_ref, xl, xh, yl, yh, next_ref):
    inflow = flow_in(now_ref[...], faces_ref, xl, xh, yl, yh)
    next_ref[...] = (sums_ref[1] + inflow) * sums_ref[0]


def tile_third(recv_ref, now_ref, sums_ref, base_ref, faces_ref, cells_ref, xl, xh, yl, yh,
               out_ref, next_ref, last_ref, cell_hot, spread, values, found):
    turned = load_slots(recv_ref, 0, 1)
    values[0] = turned[:PAD_RANKS]
    values[1] = turned[PAD_RANKS : 2 * PAD_RANKS]
    pushed, partial = scatter_cells(values, 2, cells_ref, cell_hot, spread)
    now = now_ref[...]
    inflow = flow_in(now, faces_ref, xl, xh, yl, yh)
    later = (base_ref[1] + inflow + pushed) * sums_ref[0]
    next_ref[...] = later
    last_ref[...] = base_ref[1] + partial + now * sums_ref[2]
    found[...] = jnp.zeros_like(found)
    gather_cells([now, later], cells_ref, cell_hot, found)
    store_slots(out_ref, found[...], 0, 1)


def tile_last(now_ref, last_ref, sums_ref, faces_ref, xl, xh, yl, yh, out_ref):
    inflow = flow_in(now_ref[...], faces_ref, xl, xh, yl, yh)
    out_ref[...] = (last_ref[...] + inflow) * sums_ref[0]


def ring(block, axis, step):
    count = lax.axis_size(axis)
    return lax.ppermute(block, axis, [(i, (i + step) % count) for i in range(count)])


def halo(field):
    return (
        ring(field[..., -1, :, :], "flow", 1),
        ring(field[..., 0, :, :], "flow", -1),
        ring(field[..., :, -1, :], "cross", 1),
        ring(field[..., :, 0, :], "cross", -1),
    )


def deliver(payload):
    return lax.all_to_all(payload, ("flow", "cross"), split_axis=0, concat_axis=0, tiled=True)


def on_device(
    matrix_start,
    storage,
    perm,
    frac_start,
    frac_store,
    frac_cond,
    segment_ids,
    block_counts,
    hit_tile,
    hit_cell,
    hit_weight,
):
    n_flow = lax.axis_size("flow")
    n_cross = lax.axis_size("cross")
    i_flow = lax.axis_index("flow")
    i_cross = lax.axis_index("cross")
    blocks = frac_start.shape[0]
    nx, ny, nz = matrix_start.shape
    rows = nx * ny
    flat = lambda a: a.reshape(rows, nz)
    cube = lambda a: a.reshape(nx, ny, nz)

    hits, coef, slots = call(
        owner_first,
        (shape(512, 128), shape(5, blocks, LANES), shape(2, blocks, LANES, dtype=I32)),
        8,
        scratch=[
            pltpu.VMEM((blocks, LANES, LANES), BF16),
            pltpu.VMEM((blocks, 10 * PAD_RANKS, LANES), BF16),
            pltpu.VMEM((5, blocks, LANES), F32),
        ],
        smem=(0,),
    )(
        block_counts,
        frac_start,
        frac_store,
        frac_cond,
        segment_ids,
        hit_tile.reshape(blocks, LANES),
        hit_cell,
        hit_weight,
    )
    hits = deliver(hits)
    around = halo(jnp.stack([perm, matrix_start]))
    edges = jnp.stack(
        [i_flow, n_flow - 1 - i_flow, i_cross, n_cross - 1 - i_cross]
    ).astype(I32)
    start = flat(matrix_start)
    faces, base = call(
        rock, (shape(6, rows, nz), shape(3, rows, nz)), 8, smem=(0,)
    )(edges, flat(perm), start, flat(storage), *around)

    tile_scratch = lambda count: [
        pltpu.VMEM((HALF_RANKS, LANES, LANES), BF16),
        pltpu.VMEM((HALF_RANKS, 2 * count * ROWS, LANES), BF16),
        pltpu.VMEM((count, PAD_RANKS, LANES), F32),
        pltpu.VMEM((2 * PAD_RANKS, LANES), F32),
    ]
    seen, first, sums, cells = call(
        tile_first,
        (
            shape(256, 128),
            shape(rows, nz),
            shape(3, rows, nz),
            shape(2, PAD_RANKS, LANES, dtype=I32),
        ),
        3,
        scratch=tile_scratch(4),
    )(hits, start, base)
    seen = deliver(seen)
    second = call(tile_second, shape(rows, nz), 7)(first, sums, faces, *halo(cube(first)))

    pushed, partial = call(
        owner_middle,
        (shape(256, 128), shape(blocks, LANES)),
        4,
        scratch=[
            pltpu.VMEM((blocks, LANES, LANES), BF16),
            pltpu.VMEM((blocks, 4 * PAD_RANKS, LANES), BF16),
            pltpu.VMEM((2, blocks, LANES), F32),
            pltpu.VMEM((2, blocks, LANES), F32),
        ],
    )(seen, frac_start, coef, slots)
    pushed = deliver(pushed)

    seen, third, last = call(
        tile_third,
        (shape(256, 128), shape(rows, nz), shape(rows, nz)),
        10,
        scratch=tile_scratch(2),
    )(pushed, second, sums, base, faces, cells, *halo(cube(second)))
    seen = deliver(seen)
    fourth = call(tile_last, shape(rows, nz), 8)(third, last, sums, faces, *halo(cube(third)))
    frac = call(
        owner_last,
        shape(blocks, LANES),
        4,
        scratch=[pltpu.VMEM((2, blocks, LANES), F32)],
    )(seen, coef, slots, partial)
    return cube(fourth), frac


def solution(mesh):
    grid = P("flow", "cross", None)
    owner = P(("flow", "cross"), None)
    in_specs = (grid,) * 3 + (owner,) * 4 + (P(("flow", "cross")), P(("flow", "cross"), None, None), owner, owner)
    return jax.shard_map(
        on_device, mesh=mesh, in_specs=in_specs, out_specs=(grid, owner), check_vma=False
    )
```

```python
import jax
import jax.numpy as jnp
from jax import lax
from jax.experimental import pallas as pl
from jax.experimental.pallas import tpu as pltpu
from jax.sharding import PartitionSpec as P

F32 = jnp.float32
BF16 = jnp.bfloat16
I32 = jnp.int32
I16 = jnp.int16

LANES = 256
HALF_RANKS = 36
PAD_RANKS = 40
ROWS = 64
VMEM_LIMIT = 40 * 1024 * 1024

NN = (((1,), (0,)), ((), ()))
NT = (((1,), (1,)), ((), ()))


def call(body, out_shape, n_in, scratch=(), smem=(), remote=(), microseconds=1):
    def place(i):
        if i in smem:
            return pltpu.SMEM
        return pl.ANY if i in remote else pltpu.VMEM

    out_specs = jax.tree.map(lambda _: pl.BlockSpec(memory_space=pltpu.VMEM), out_shape)
    return pl.pallas_call(
        body,
        out_shape=out_shape,
        in_specs=[pl.BlockSpec(memory_space=place(i)) for i in range(n_in)],
        out_specs=out_specs,
        scratch_shapes=list(scratch),
        compiler_params=pltpu.CompilerParams(vmem_limit_bytes=VMEM_LIMIT),
        cost_estimate=pl.CostEstimate(
            flops=0, bytes_accessed=int(microseconds * 3_000_000), transcendentals=0
        ),
    )


def shape(*dims, dtype=F32):
    return jax.ShapeDtypeStruct(dims, dtype)


def halves(value):
    high = value.astype(BF16).astype(F32)
    return high, value - high


def hot_rows(index_row, count):
    place = lax.broadcasted_iota(I16, (16, LANES), 0)
    index = jnp.broadcast_to(index_row, (16, LANES)).astype(I16)
    one, none = jnp.ones((16, LANES), BF16), jnp.zeros((16, LANES), BF16)
    return jnp.concatenate(
        [jnp.where(place == index - jnp.int16(16 * j), one, none) for j in range(count // 16)], axis=0
    )


def same(index_row, count):
    return lax.broadcasted_iota(I32, (count, LANES), 0) == index_row


def shift_right(x):
    return pltpu.roll(x, 1, 1)


def shift_left(x):
    return pltpu.roll(x, LANES - 1, 1)


def store_slots(out_ref, by_slot, group, groups):
    rows = by_slot.shape[0]
    if rows < 128:
        by_slot = jnp.concatenate([by_slot, jnp.zeros((128 - rows, LANES), F32)], axis=0)
    turned = by_slot.T
    for part in range(2):
        out_ref[pl.ds(group * 2 + part, 128, stride=2 * groups), :] = turned[
            part * 128 : part * 128 + 128
        ]


def load_slots(in_ref, group, groups):
    parts = [in_ref[pl.ds(group * 2 + part, 128, stride=2 * groups), :] for part in range(2)]
    return jnp.concatenate(parts, axis=0).T


def spread_ranks(split, b, rank_half):
    mine = same(rank_half, PAD_RANKS)
    rows = [jnp.where(mine, split[v, b : b + 1, :], 0.0) for v in range(split.shape[0])]
    return jnp.concatenate(rows, axis=0).astype(BF16)


def joined(total, height, count):
    return [
        total[2 * v * height : (2 * v + 1) * height] + total[(2 * v + 1) * height : (2 * v + 2) * height]
        for v in range(count)
    ]


def put_split(split, v, value):
    high, low = halves(value)
    split[2 * v] = high
    split[2 * v + 1] = low


def owner_first(
    count_ref, start_hbm, store_hbm, cond_hbm, seg_hbm, tile_hbm, cell_hbm, weight_hbm,
    out_ref, coef_ref, slot_ref,
    start_ref, store_ref, cond_ref, seg_ref, tile_ref, cell_ref, weight_ref, arrived, split,
):
    pairs = [
        (tile_hbm, tile_ref), (seg_hbm, seg_ref), (cond_hbm, cond_ref), (weight_hbm, weight_ref),
        (store_hbm, store_ref), (start_hbm, start_ref), (cell_hbm, cell_ref),
    ]
    copies = [pltpu.make_async_copy(a, b, arrived.at[i]) for i, (a, b) in enumerate(pairs)]
    for copy in copies:
        copy.start()
    for copy in copies:
        copy.wait()
    blocks = start_ref.shape[0]
    size = (blocks, LANES)
    live = lax.broadcasted_iota(I32, size, 0) < count_ref[0]
    lane = lax.broadcasted_iota(I32, size, 1)
    start = start_ref[...]
    store = store_ref[...]
    weight = jnp.where(live, weight_ref[...], 0.0)
    seg = seg_ref[...]
    linked = (seg == shift_left(seg)) & (lane < LANES - 1)
    right = jnp.where(linked, cond_ref[...], 0.0)
    left = shift_right(right)
    inverse = 1.0 / (store + left + right + weight)
    own = jnp.where(live, store * start * inverse, start)
    left = jnp.where(live, left * inverse, 0.0)
    right = jnp.where(live, right * inverse, 0.0)
    pull = weight * inverse
    coef_ref[0] = own
    coef_ref[1] = left
    coef_ref[2] = right
    coef_ref[3] = pull
    coef_ref[4] = weight
    partial = own + left * shift_right(start) + right * shift_left(start)
    put_split(split, 0, cell_ref[...].astype(F32))
    put_split(split, 1, weight)
    put_split(split, 2, weight * start)
    put_split(split, 3, weight * partial)
    put_split(split, 4, weight * pull)
    tile = jnp.concatenate(
        [tile_ref[pl.ds(0, blocks, stride=2), :], tile_ref[pl.ds(1, blocks, stride=2), :]], axis=1
    )
    slot_ref[0] = jnp.where(live, tile, -1)
    upper = jnp.where(
        lax.broadcasted_iota(I32, (LANES, LANES), 0) <= lax.broadcasted_iota(I32, (LANES, LANES), 1),
        1.0, 0.0,
    ).astype(BF16)
    before = jnp.zeros((128, LANES), F32)
    total = jnp.zeros((10 * PAD_RANKS, LANES), F32)
    for b in range(blocks):
        target = slot_ref[0, b : b + 1, :]
        mine = same(target, 128)
        running = lax.dot_general(
            jnp.where(mine, 1.0, 0.0).astype(BF16), upper, NN, preferred_element_type=F32
        )
        rank = jnp.sum(jnp.where(mine, running + before, 0.0), axis=0, keepdims=True).astype(I32) - 1
        before += jnp.broadcast_to(running[:, LANES - 1 :], (128, LANES))
        rank = jnp.maximum(rank, 0)
        key = jnp.where(target >= 0, target + (rank & 1) * 128, -1)
        rank_half = rank >> 1
        slot_ref[0, b : b + 1, :] = key
        slot_ref[1, b : b + 1, :] = rank_half
        total += lax.dot_general(
            spread_ranks(split, b, rank_half), hot_rows(key, LANES), NT, preferred_element_type=F32
        )
    sums = joined(total, PAD_RANKS, 5)
    store_slots(out_ref, jnp.concatenate(sums[:3], axis=0), 0, 2)
    store_slots(out_ref, jnp.concatenate(sums[3:], axis=0), 1, 2)


def unpack(recv_ref, slot_ref, key_hot, seen, blocks):
    turned = load_slots(recv_ref, 0, 1)[: 2 * PAD_RANKS]
    table = jnp.concatenate(halves(turned), axis=0).astype(BF16)
    for b in range(blocks):
        hot = hot_rows(slot_ref[0, b : b + 1, :], LANES)
        if key_hot is not None:
            key_hot[b] = hot
        found = lax.dot_general(table, hot, NN, preferred_element_type=F32)
        found = found[: 2 * PAD_RANKS] + found[2 * PAD_RANKS :]
        mine = same(slot_ref[1, b : b + 1, :], PAD_RANKS)
        for v in range(2):
            part = jnp.where(mine, found[v * PAD_RANKS : (v + 1) * PAD_RANKS], 0.0)
            seen[v, b : b + 1, :] = jnp.sum(part, axis=0, keepdims=True)


def owner_middle(
    recv_ref, start_ref, coef_ref, slot_ref, out_ref, partial_ref, key_hot, seen, split
):
    blocks = start_ref.shape[0]
    unpack(recv_ref, slot_ref, key_hot, seen, blocks)
    own, left, right, pull, weight = [coef_ref[i] for i in range(5)]
    now = start_ref[...]
    for v in range(2):
        now = own + left * shift_right(now) + right * shift_left(now) + pull * seen[v]
    partial = own + left * shift_right(now) + right * shift_left(now)
    partial_ref[...] = partial
    put_split(split, 0, weight * now)
    put_split(split, 1, weight * partial)
    total = jnp.zeros((4 * PAD_RANKS, LANES), F32)
    for b in range(blocks):
        total += lax.dot_general(
            spread_ranks(split, b, slot_ref[1, b : b + 1, :]), key_hot[b], NT,
            preferred_element_type=F32,
        )
    store_slots(out_ref, jnp.concatenate(joined(total, PAD_RANKS, 2), axis=0), 0, 1)


def owner_last(recv_ref, coef_ref, slot_ref, partial_ref, out_ref, seen):
    blocks = partial_ref.shape[0]
    unpack(recv_ref, slot_ref, None, seen, blocks)
    own, left, right, pull = [coef_ref[i] for i in range(4)]
    now = partial_ref[...] + pull * seen[0]
    out_ref[...] = own + left * shift_right(now) + right * shift_left(now) + pull * seen[1]


def fold(field):
    return jnp.concatenate([field[:, :LANES], field[:, LANES:]], axis=0)


def unfold(rows):
    half = ROWS // 2
    return jnp.concatenate([rows[:half], rows[half:]], axis=1)


def gather_cells(fields, cell_ref, found_ref):
    parts = []
    for field in fields:
        parts += halves(fold(field))
    table = jnp.concatenate(parts, axis=0).astype(BF16)
    for r in range(HALF_RANKS):
        mine = same(cell_ref[0, r : r + 1, :], ROWS)
        hot = hot_rows(cell_ref[1, r : r + 1, :], LANES)
        found = lax.dot_general(table, hot, NN, preferred_element_type=F32)
        for v, both in enumerate(joined(found, ROWS, len(fields))):
            found_ref[v * PAD_RANKS + r : v * PAD_RANKS + r + 1, :] = jnp.sum(
                jnp.where(mine, both, 0.0), axis=0, keepdims=True
            )


def scatter_cells(split, count, cell_ref, sums_ref):
    place = lax.broadcasted_iota(I16, (16, LANES), 0)
    none = jnp.zeros((16, LANES), BF16)
    total = jnp.zeros((2 * count * ROWS, LANES), F32)
    for r in range(HALF_RANKS):
        row = jnp.broadcast_to(cell_ref[0, r : r + 1, :], (16, LANES)).astype(I16)
        mine = [place == row - jnp.int16(16 * j) for j in range(ROWS // 16)]
        rows = []
        for v in range(2 * count):
            value = jnp.broadcast_to(split[v, r : r + 1, :], (16, LANES)).astype(BF16)
            rows += [jnp.where(m, value, none) for m in mine]
        hot = hot_rows(cell_ref[1, r : r + 1, :], LANES)
        total += lax.dot_general(
            jnp.concatenate(rows, axis=0), hot, NT, preferred_element_type=F32
        )
    for v, both in enumerate(joined(total, ROWS, count)):
        sums_ref[v] = unfold(both)


def put_faces(field, refs):
    rows = field.shape[0]
    refs[0][...] = field[rows - 8 :]
    refs[1][...] = field[:8]
    refs[2][...] = jnp.concatenate([field[i + 7 : i + 8] for i in range(0, rows, 8)], axis=0)
    refs[3][...] = jnp.concatenate([field[i : i + 1] for i in range(0, rows, 8)], axis=0)


def rock_faces(perm_ref, start_ref, a, b, c, d):
    perm, start = perm_ref[...], start_ref[...]
    rows = perm.shape[0]
    for i, field in enumerate((perm, start)):
        a[i * 8 : i * 8 + 8, :] = field[rows - 8 :]
        b[i * 8 : i * 8 + 8, :] = field[:8]
    c[...] = jnp.concatenate(
        [f[i + 7 : i + 8] for f in (perm, start) for i in range(0, rows, 8)], axis=0
    )
    d[...] = jnp.concatenate(
        [f[i : i + 1] for f in (perm, start) for i in range(0, rows, 8)], axis=0
    )


def neighbours(field, x_low, x_high, y_low, y_high, ny):
    rows, nz = field.shape
    nx = rows // ny
    west = jnp.concatenate([x_low, field[: rows - ny]], axis=0)
    east = jnp.concatenate([field[ny:], x_high], axis=0)
    place = lax.broadcasted_iota(I32, (rows, nz), 0) % ny
    wide_low = jnp.concatenate(
        [jnp.broadcast_to(y_low[i : i + 1], (ny, nz)) for i in range(nx)], axis=0
    )
    wide_high = jnp.concatenate(
        [jnp.broadcast_to(y_high[i : i + 1], (ny, nz)) for i in range(nx)], axis=0
    )
    south = jnp.where(place == 0, wide_low, pltpu.roll(field, 1, 0))
    north = jnp.where(place == ny - 1, wide_high, pltpu.roll(field, rows - 1, 0))
    below = pltpu.roll(field, 1, 1)
    above = pltpu.roll(field, nz - 1, 1)
    return west, east, south, north, below, above


def tile_scatter(recv_ref, sums_ref, cells_ref, split):
    first = load_slots(recv_ref, 0, 2)
    second = load_slots(recv_ref, 1, 2)
    cell = first[:PAD_RANKS].astype(I32)
    deep = cell & 511
    cells_ref[0] = ((deep >> 8) << 5) + (cell >> 9)
    cells_ref[1] = deep & (LANES - 1)
    put_split(split, 0, first[PAD_RANKS : 2 * PAD_RANKS])
    put_split(split, 1, first[2 * PAD_RANKS : 3 * PAD_RANKS])
    put_split(split, 2, second[:PAD_RANKS])
    put_split(split, 3, second[PAD_RANKS : 2 * PAD_RANKS])
    scatter_cells(split, 4, cells_ref, sums_ref)


def tile_first(edge_ref, hits_ref, cells_ref, perm_ref, start_ref, storage_ref, xl, xh, yl, yh,
               out_ref, next_ref, sums_ref, faces_ref, a, b, c, d, found):
    rows, nz = perm_ref.shape
    ny = 8
    perm = perm_ref[...]
    start = start_ref[...]
    nx = rows // ny
    beside = neighbours(perm, xl[:8], xh[:8], yl[:nx], yh[:nx], ny)
    around = neighbours(start, xl[8:], xh[8:], yl[nx:], yh[nx:], ny)
    row = lax.broadcasted_iota(I32, (rows, nz), 0)
    lane = lax.broadcasted_iota(I32, (rows, nz), 1)
    closed = [
        (row < ny) & (edge_ref[0] == 0),
        (row >= rows - ny) & (edge_ref[1] == 0),
        (row % ny == 0) & (edge_ref[2] == 0),
        (row % ny == ny - 1) & (edge_ref[3] == 0),
        lane == 0,
        lane == nz - 1,
    ]
    storage = storage_ref[...]
    base = storage * start
    inflow = jnp.zeros_like(start)
    total = storage + hits_ref[0]
    for i in range(6):
        face = jnp.where(closed[i], 0.0, 2.0 * perm * beside[i] / (perm + beside[i]))
        faces_ref[i] = face
        total += face
        inflow += face * around[i]
    inverse = 1.0 / total
    now = (base + inflow + hits_ref[1]) * inverse
    next_ref[...] = now
    put_faces(now, (a, b, c, d))
    sums_ref[0] = inverse
    sums_ref[1] = base
    sums_ref[2] = base + hits_ref[2] + start * hits_ref[3]
    sums_ref[3] = hits_ref[3]
    found[...] = jnp.zeros_like(found)
    gather_cells([start, now], cells_ref, found)
    store_slots(out_ref, found[...], 0, 1)


def flow_in(field, faces_ref, xl, xh, yl, yh):
    around = neighbours(field, xl[...], xh[...], yl[...], yh[...], 8)
    total = faces_ref[0] * around[0]
    for i in range(1, 6):
        total += faces_ref[i] * around[i]
    return total


def tile_second(now_ref, sums_ref, faces_ref, xl, xh, yl, yh, after, next_ref, a, b, c, d):
    inflow = flow_in(now_ref[...], faces_ref, xl, xh, yl, yh)
    later = (sums_ref[2] + inflow) * sums_ref[0]
    next_ref[...] = later
    put_faces(later, (a, b, c, d))


def tile_scatter_again(recv_ref, cells_ref, sums_ref, split):
    turned = load_slots(recv_ref, 0, 1)
    put_split(split, 0, turned[:PAD_RANKS])
    put_split(split, 1, turned[PAD_RANKS : 2 * PAD_RANKS])
    scatter_cells(split, 2, cells_ref, sums_ref)


def tile_third(hits_ref, now_ref, sums_ref, faces_ref, cells_ref, xl, xh, yl, yh,
               out_ref, next_ref, last_ref, a, b, c, d, found):
    now = now_ref[...]
    inflow = flow_in(now, faces_ref, xl, xh, yl, yh)
    later = (sums_ref[1] + inflow + hits_ref[0]) * sums_ref[0]
    next_ref[...] = later
    put_faces(later, (a, b, c, d))
    last_ref[...] = sums_ref[1] + hits_ref[1] + now * sums_ref[3]
    found[...] = jnp.zeros_like(found)
    gather_cells([now, later], cells_ref, found)
    store_slots(out_ref, found[...], 0, 1)


def tile_last(now_ref, last_ref, sums_ref, faces_ref, xl, xh, yl, yh, after, out_ref):
    inflow = flow_in(now_ref[...], faces_ref, xl, xh, yl, yh)
    out_ref[...] = (last_ref[...] + inflow) * sums_ref[0]


def ring(block, axis, step):
    count = lax.axis_size(axis)
    return lax.ppermute(block, axis, [(i, (i + step) % count) for i in range(count)])


def swap(faces):
    return (
        ring(faces[0], "flow", 1),
        ring(faces[1], "flow", -1),
        ring(faces[2], "cross", 1),
        ring(faces[3], "cross", -1),
    )


def deliver(payload):
    return lax.all_to_all(payload, ("flow", "cross"), split_axis=0, concat_axis=0, tiled=True)


def on_device(
    matrix_start, storage, perm, frac_start, frac_store, frac_cond,
    segment_ids, block_counts, hit_tile, hit_cell, hit_weight,
):
    n_flow, n_cross = lax.axis_size("flow"), lax.axis_size("cross")
    i_flow, i_cross = lax.axis_index("flow"), lax.axis_index("cross")
    blocks = frac_start.shape[0]
    nx, ny, nz = matrix_start.shape
    rows = nx * ny
    start, storage, perm = [a.reshape(rows, nz) for a in (matrix_start, storage, perm)]
    field = shape(rows, nz)
    faces_of = lambda n: (shape(n * ny, nz), shape(n * ny, nz), shape(n * nx, nz), shape(n * nx, nz))
    owned = lambda dtype: pltpu.VMEM((blocks, LANES), dtype)
    edges = jnp.stack([i_flow, n_flow - 1 - i_flow, i_cross, n_cross - 1 - i_cross]).astype(I32)

    hits, coef, slots = call(
        owner_first,
        (shape(512, 128), shape(5, blocks, LANES), shape(2, blocks, LANES, dtype=I32)),
        8,
        scratch=[
            owned(F32), owned(F32), owned(F32), owned(I32),
            pltpu.VMEM((2 * blocks, 128), I32), owned(I32), owned(F32),
            pltpu.SemaphoreType.DMA((7,)),
            pltpu.VMEM((10, blocks, LANES), F32),
        ],
        smem=(0,),
        remote=range(1, 8),
        microseconds=6,
    )(
        block_counts, frac_start, frac_store, frac_cond, segment_ids,
        hit_tile.reshape(2 * blocks, 128), hit_cell, hit_weight,
    )
    hits = deliver(hits)
    around = swap(call(rock_faces, faces_of(2), 2)(perm, start))
    sums, cells = call(
        tile_scatter,
        (shape(4, rows, nz), shape(2, PAD_RANKS, LANES, dtype=I32)),
        1,
        scratch=[pltpu.VMEM((8, PAD_RANKS, LANES), F32)],
        microseconds=4,
    )(hits)
    found = pltpu.VMEM((2 * PAD_RANKS, LANES), F32)
    seen, first, sums, faces, *sides = call(
        tile_first,
        (shape(256, 128), field, shape(4, rows, nz), shape(6, rows, nz)) + faces_of(1),
        10,
        scratch=[found],
        smem=(0,),
        microseconds=4,
    )(edges, sums, cells, perm, start, storage, *around)
    seen = deliver(seen)
    around = swap(sides)

    pushed, partial = call(
        owner_middle,
        (shape(256, 128), shape(blocks, LANES)),
        4,
        scratch=[
            pltpu.VMEM((blocks, LANES, LANES), BF16),
            pltpu.VMEM((2, blocks, LANES), F32),
            pltpu.VMEM((4, blocks, LANES), F32),
        ],
        microseconds=5,
    )(seen, frac_start, coef, slots)
    pushed = deliver(pushed)
    second, *sides = call(tile_second, (field,) + faces_of(1), 8, remote=(7,))(
        first, sums, faces, *around, partial
    )
    around = swap(sides)

    hits = call(
        tile_scatter_again,
        shape(2, rows, nz),
        2,
        scratch=[pltpu.VMEM((4, PAD_RANKS, LANES), F32)],
        microseconds=3,
    )(pushed, cells)
    seen, third, last, *sides = call(
        tile_third,
        (shape(256, 128), field, field) + faces_of(1),
        9,
        scratch=[found],
        microseconds=4,
    )(hits, second, sums, faces, cells, *around)
    seen = deliver(seen)
    around = swap(sides)
    frac = call(
        owner_last,
        shape(blocks, LANES),
        4,
        scratch=[pltpu.VMEM((2, blocks, LANES), F32)],
        microseconds=4,
    )(seen, coef, slots, partial)
    fourth = call(tile_last, field, 9, remote=(8,))(third, last, sums, faces, *around, frac)
    return fourth.reshape(nx, ny, nz), frac


def solution(mesh):
    grid = P("flow", "cross", None)
    owner = P(("flow", "cross"), None)
    counts, tiles = P(("flow", "cross")), P(("flow", "cross"), None, None)
    in_specs = (grid,) * 3 + (owner,) * 4 + (counts, tiles, owner, owner)
    return jax.shard_map(
        on_device, mesh=mesh, in_specs=in_specs, out_specs=(grid, owner), check_vma=False
    )
```

```python
import jax
import jax.numpy as jnp
from jax import lax
from jax.experimental import pallas as pl
from jax.experimental.pallas import tpu as pltpu
from jax.sharding import PartitionSpec as P

F32 = jnp.float32
BF16 = jnp.bfloat16
I32 = jnp.int32
I16 = jnp.int16

LANES = 256
HALF_RANKS = 36
PAD_RANKS = 40
ROWS = 64
VMEM_LIMIT = 40 * 1024 * 1024

NN = (((1,), (0,)), ((), ()))
NT = (((1,), (1,)), ((), ()))


def call(body, out_shape, n_in, scratch=(), smem=(), remote=(), microseconds=1, vmem=VMEM_LIMIT):
    def place(i):
        if i in smem:
            return pltpu.SMEM
        return pltpu.HBM if i in remote else pltpu.VMEM

    out_specs = jax.tree.map(lambda _: pl.BlockSpec(memory_space=pltpu.VMEM), out_shape)
    return pl.pallas_call(
        body,
        out_shape=out_shape,
        in_specs=[pl.BlockSpec(memory_space=place(i)) for i in range(n_in)],
        out_specs=out_specs,
        scratch_shapes=list(scratch),
        compiler_params=pltpu.CompilerParams(vmem_limit_bytes=vmem),
        cost_estimate=pl.CostEstimate(
            flops=0, bytes_accessed=int(microseconds * 3_000_000), transcendentals=0
        ),
    )


def shape(*dims, dtype=F32):
    return jax.ShapeDtypeStruct(dims, dtype)


def halves(value):
    high = value.astype(BF16).astype(F32)
    return high, value - high


def hot_rows(index_row, count):
    place = lax.broadcasted_iota(I16, (16, LANES), 0)
    index = jnp.broadcast_to(index_row, (16, LANES)).astype(I16)
    one, none = jnp.ones((16, LANES), BF16), jnp.zeros((16, LANES), BF16)
    return jnp.concatenate(
        [jnp.where(place == index - jnp.int16(16 * j), one, none) for j in range(count // 16)], axis=0
    )


def same(index_row, count):
    return lax.broadcasted_iota(I32, (count, LANES), 0) == index_row


def shift_right(x):
    return pltpu.roll(x, 1, 1)


def shift_left(x):
    return pltpu.roll(x, LANES - 1, 1)


def store_slots(out_ref, by_slot, group, groups):
    rows = by_slot.shape[0]
    if rows < 128:
        by_slot = jnp.concatenate([by_slot, jnp.zeros((128 - rows, LANES), F32)], axis=0)
    turned = by_slot.T
    for part in range(2):
        out_ref[pl.ds(group * 2 + part, 128, stride=2 * groups), :] = turned[
            part * 128 : part * 128 + 128
        ]


def load_slots(in_ref, group, groups):
    parts = [in_ref[pl.ds(group * 2 + part, 128, stride=2 * groups), :] for part in range(2)]
    return jnp.concatenate(parts, axis=0).T


def spread_ranks(split, b, rank_half):
    mine = same(rank_half, PAD_RANKS)
    rows = [jnp.where(mine, split[v, b : b + 1, :], 0.0) for v in range(split.shape[0])]
    return jnp.concatenate(rows, axis=0).astype(BF16)


def joined(total, height, count):
    return [
        total[2 * v * height : (2 * v + 1) * height] + total[(2 * v + 1) * height : (2 * v + 2) * height]
        for v in range(count)
    ]


def put_split(split, v, value):
    high, low = halves(value)
    split[2 * v] = high
    split[2 * v + 1] = low


def owner_first(
    count_ref, start_hbm, store_hbm, cond_hbm, seg_hbm, tile_hbm, cell_hbm, weight_hbm,
    out_ref, coef_ref, slot_ref,
    start_ref, store_ref, cond_ref, seg_ref, tile_ref, cell_ref, weight_ref, arrived, split,
):
    pairs = [
        (tile_hbm, tile_ref), (seg_hbm, seg_ref), (cond_hbm, cond_ref), (weight_hbm, weight_ref),
        (store_hbm, store_ref), (start_hbm, start_ref), (cell_hbm, cell_ref),
    ]
    copies = [pltpu.make_async_copy(a, b, arrived.at[i]) for i, (a, b) in enumerate(pairs)]
    for copy in copies:
        copy.start()
    for copy in copies:
        copy.wait()
    blocks = start_ref.shape[0]
    size = (blocks, LANES)
    live = lax.broadcasted_iota(I32, size, 0) < count_ref[0]
    lane = lax.broadcasted_iota(I32, size, 1)
    start = start_ref[...]
    store = store_ref[...]
    weight = jnp.where(live, weight_ref[...], 0.0)
    seg = seg_ref[...]
    linked = (seg == shift_left(seg)) & (lane < LANES - 1)
    right = jnp.where(linked, cond_ref[...], 0.0)
    left = shift_right(right)
    inverse = 1.0 / (store + left + right + weight)
    own = jnp.where(live, store * start * inverse, start)
    left = jnp.where(live, left * inverse, 0.0)
    right = jnp.where(live, right * inverse, 0.0)
    pull = weight * inverse
    coef_ref[0] = own
    coef_ref[1] = left
    coef_ref[2] = right
    coef_ref[3] = pull
    coef_ref[4] = weight
    partial = own + left * shift_right(start) + right * shift_left(start)
    put_split(split, 0, cell_ref[...].astype(F32))
    put_split(split, 1, weight)
    put_split(split, 2, weight * start)
    put_split(split, 3, weight * partial)
    put_split(split, 4, weight * pull)
    tile = jnp.concatenate(
        [tile_ref[pl.ds(0, blocks, stride=2), :], tile_ref[pl.ds(1, blocks, stride=2), :]], axis=1
    )
    slot_ref[0] = jnp.where(live, tile, -1)
    upper = jnp.where(
        lax.broadcasted_iota(I32, (LANES, LANES), 0) <= lax.broadcasted_iota(I32, (LANES, LANES), 1),
        1.0, 0.0,
    ).astype(BF16)
    before = jnp.zeros((128, LANES), F32)
    for b in range(blocks):
        target = slot_ref[0, b : b + 1, :]
        mine = same(target, 128)
        running = lax.dot_general(
            jnp.where(mine, 1.0, 0.0).astype(BF16), upper, NN, preferred_element_type=F32
        )
        rank = jnp.sum(jnp.where(mine, running + before, 0.0), axis=0, keepdims=True).astype(I32) - 1
        before += jnp.broadcast_to(running[:, LANES - 1 :], (128, LANES))
        slot_ref[1, b : b + 1, :] = jnp.maximum(rank, 0)
    target, rank = slot_ref[0], slot_ref[1]
    slot_ref[0] = jnp.where(live, target + (rank & 1) * 128, -1)
    slot_ref[1] = rank >> 1
    total = jnp.zeros((10 * PAD_RANKS, LANES), F32)
    for b in range(blocks):
        total += lax.dot_general(
            spread_ranks(split, b, slot_ref[1, b : b + 1, :]),
            hot_rows(slot_ref[0, b : b + 1, :], LANES), NT, preferred_element_type=F32,
        )
    sums = joined(total, PAD_RANKS, 5)
    store_slots(out_ref, jnp.concatenate(sums[:3], axis=0), 0, 2)
    store_slots(out_ref, jnp.concatenate(sums[3:], axis=0), 1, 2)


def unpack(recv_ref, slot_ref, key_hot, seen, blocks):
    turned = load_slots(recv_ref, 0, 1)[: 2 * PAD_RANKS]
    table = jnp.concatenate(halves(turned), axis=0).astype(BF16)
    for b in range(blocks):
        hot = hot_rows(slot_ref[0, b : b + 1, :], LANES)
        if key_hot is not None:
            key_hot[b] = hot
        found = lax.dot_general(table, hot, NN, preferred_element_type=F32)
        found = found[: 2 * PAD_RANKS] + found[2 * PAD_RANKS :]
        mine = same(slot_ref[1, b : b + 1, :], PAD_RANKS)
        for v in range(2):
            part = jnp.where(mine, found[v * PAD_RANKS : (v + 1) * PAD_RANKS], 0.0)
            seen[v, b : b + 1, :] = jnp.sum(part, axis=0, keepdims=True)


def owner_middle(
    recv_ref, start_ref, coef_ref, slot_ref, yh, xh, yl, xl, out_ref, partial_ref, key_hot, seen, split
):
    blocks = start_ref.shape[0]
    unpack(recv_ref, slot_ref, key_hot, seen, blocks)
    own, left, right, pull, weight = [coef_ref[i] for i in range(5)]
    now = start_ref[...]
    for v in range(2):
        now = own + left * shift_right(now) + right * shift_left(now) + pull * seen[v]
    partial = own + left * shift_right(now) + right * shift_left(now)
    partial_ref[...] = partial
    put_split(split, 0, weight * now)
    put_split(split, 1, weight * partial)
    total = jnp.zeros((4 * PAD_RANKS, LANES), F32)
    for b in range(blocks):
        total += lax.dot_general(
            spread_ranks(split, b, slot_ref[1, b : b + 1, :]), key_hot[b], NT,
            preferred_element_type=F32,
        )
    store_slots(out_ref, jnp.concatenate(joined(total, PAD_RANKS, 2), axis=0), 0, 1)


def owner_last(recv_ref, coef_ref, slot_ref, partial_ref, out_ref, token_ref, seen):
    token_ref[...] = jnp.zeros_like(token_ref)
    blocks = partial_ref.shape[0]
    unpack(recv_ref, slot_ref, None, seen, blocks)
    own, left, right, pull = [coef_ref[i] for i in range(4)]
    now = partial_ref[...] + pull * seen[0]
    out_ref[...] = own + left * shift_right(now) + right * shift_left(now) + pull * seen[1]


def fold(field):
    return jnp.concatenate([field[:, :LANES], field[:, LANES:]], axis=0)


def unfold(rows):
    half = ROWS // 2
    return jnp.concatenate([rows[:half], rows[half:]], axis=1)


def gather_cells(fields, cell_ref, found_ref):
    parts = []
    for field in fields:
        parts += halves(fold(field))
    table = jnp.concatenate(parts, axis=0).astype(BF16)
    for r in range(HALF_RANKS):
        mine = same(cell_ref[0, r : r + 1, :], ROWS)
        hot = hot_rows(cell_ref[1, r : r + 1, :], LANES)
        found = lax.dot_general(table, hot, NN, preferred_element_type=F32)
        for v, both in enumerate(joined(found, ROWS, len(fields))):
            found_ref[v * PAD_RANKS + r : v * PAD_RANKS + r + 1, :] = jnp.sum(
                jnp.where(mine, both, 0.0), axis=0, keepdims=True
            )


def scatter_cells(split, count, cell_ref, sums_ref):
    place = lax.broadcasted_iota(I16, (16, LANES), 0)
    none = jnp.zeros((16, LANES), BF16)
    total = jnp.zeros((2 * count * ROWS, LANES), F32)
    for r in range(HALF_RANKS):
        row = jnp.broadcast_to(cell_ref[0, r : r + 1, :], (16, LANES)).astype(I16)
        mine = [place == row - jnp.int16(16 * j) for j in range(ROWS // 16)]
        rows = []
        for v in range(2 * count):
            value = jnp.broadcast_to(split[v, r : r + 1, :], (16, LANES)).astype(BF16)
            rows += [jnp.where(m, value, none) for m in mine]
        hot = hot_rows(cell_ref[1, r : r + 1, :], LANES)
        total += lax.dot_general(
            jnp.concatenate(rows, axis=0), hot, NT, preferred_element_type=F32
        )
    for v, both in enumerate(joined(total, ROWS, count)):
        sums_ref[v] = unfold(both)


def pick(odd, yes, no):
    return jnp.where(odd, yes, no)


def parity():
    return lax.axis_index("flow") % 2 == 1, lax.axis_index("cross") % 2 == 1


def y_faces(field):
    rows = field.shape[0]
    low = jnp.concatenate([field[i : i + 1] for i in range(0, rows, 8)], axis=0)
    high = jnp.concatenate([field[i + 7 : i + 8] for i in range(0, rows, 8)], axis=0)
    return low, high


def put_faces(field, refs, place=0):
    rows = field.shape[0]
    odd_x, odd_y = parity()
    x_low, x_high = field[:8], field[rows - 8 :]
    y_low, y_high = y_faces(field)
    at_x, at_y = pl.ds(place * 8, 8), pl.ds(place * (rows // 8), rows // 8)
    refs[0][at_x, :] = pick(odd_x, x_low, x_high)
    refs[1][at_x, :] = pick(odd_x, x_high, x_low)
    refs[2][at_y, :] = pick(odd_y, y_low, y_high)
    refs[3][at_y, :] = pick(odd_y, y_high, y_low)


def sides_of(refs, place=0, rows=32):
    odd_x, odd_y = parity()
    at_x, at_y = pl.ds(place * 8, 8), pl.ds(place * (rows // 8), rows // 8)
    x_first, x_second = refs[0][at_x, :], refs[1][at_x, :]
    y_first, y_second = refs[2][at_y, :], refs[3][at_y, :]
    return (
        pick(odd_x, x_first, x_second),
        pick(odd_x, x_second, x_first),
        pick(odd_y, y_first, y_second),
        pick(odd_y, y_second, y_first),
    )


def rock_faces(perm_ref, start_ref, *sides):
    put_faces(perm_ref[...], sides, 0)
    put_faces(start_ref[...], sides, 1)


def neighbours(field, x_low, x_high, y_low, y_high, ny):
    rows, nz = field.shape
    nx = rows // ny
    west = jnp.concatenate([x_low, field[: rows - ny]], axis=0)
    east = jnp.concatenate([field[ny:], x_high], axis=0)
    place = lax.broadcasted_iota(I32, (rows, nz), 0) % ny
    wide_low = jnp.concatenate(
        [jnp.broadcast_to(y_low[i : i + 1], (ny, nz)) for i in range(nx)], axis=0
    )
    wide_high = jnp.concatenate(
        [jnp.broadcast_to(y_high[i : i + 1], (ny, nz)) for i in range(nx)], axis=0
    )
    south = jnp.where(place == 0, wide_low, pltpu.roll(field, 1, 0))
    north = jnp.where(place == ny - 1, wide_high, pltpu.roll(field, rows - 1, 0))
    below = pltpu.roll(field, 1, 1)
    above = pltpu.roll(field, nz - 1, 1)
    return west, east, south, north, below, above


def tile_scatter(recv_ref, sums_ref, cells_ref, split):
    first = load_slots(recv_ref, 0, 2)
    second = load_slots(recv_ref, 1, 2)
    cell = first[:PAD_RANKS].astype(I32)
    deep = cell & 511
    cells_ref[0] = ((deep >> 8) << 5) + (cell >> 9)
    cells_ref[1] = deep & (LANES - 1)
    put_split(split, 0, first[PAD_RANKS : 2 * PAD_RANKS])
    put_split(split, 1, first[2 * PAD_RANKS : 3 * PAD_RANKS])
    put_split(split, 2, second[:PAD_RANKS])
    put_split(split, 3, second[PAD_RANKS : 2 * PAD_RANKS])
    scatter_cells(split, 4, cells_ref, sums_ref)


def tile_first(hits_ref, cells_ref, perm_ref, start_ref, storage_ref, yh, xh, yl, xl,
               out_ref, next_ref, sums_ref, faces_ref, a, b, c, d, found):
    rows, nz = perm_ref.shape
    ny = 8
    perm = perm_ref[...]
    start = start_ref[...]
    beside = neighbours(perm, *sides_of((xl, xh, yl, yh), 0), ny)
    around = neighbours(start, *sides_of((xl, xh, yl, yh), 1), ny)
    i_flow, i_cross = lax.axis_index("flow"), lax.axis_index("cross")
    row = lax.broadcasted_iota(I32, (rows, nz), 0)
    lane = lax.broadcasted_iota(I32, (rows, nz), 1)
    closed = [
        (row < ny) & (i_flow == 0),
        (row >= rows - ny) & (i_flow == lax.axis_size("flow") - 1),
        (row % ny == 0) & (i_cross == 0),
        (row % ny == ny - 1) & (i_cross == lax.axis_size("cross") - 1),
        lane == 0,
        lane == nz - 1,
    ]
    storage = storage_ref[...]
    base = storage * start
    inflow = jnp.zeros_like(start)
    total = storage + hits_ref[0]
    for i in range(6):
        face = jnp.where(closed[i], 0.0, 2.0 * perm * beside[i] / (perm + beside[i]))
        faces_ref[i] = face
        total += face
        inflow += face * around[i]
    inverse = 1.0 / total
    now = (base + inflow + hits_ref[1]) * inverse
    next_ref[...] = now
    put_faces(now, (a, b, c, d))
    sums_ref[0] = inverse
    sums_ref[1] = base
    sums_ref[2] = base + hits_ref[2] + start * hits_ref[3]
    sums_ref[3] = hits_ref[3]
    found[...] = jnp.zeros_like(found)
    gather_cells([start, now], cells_ref, found)
    store_slots(out_ref, found[...], 0, 1)


def flow_in(field, faces_ref, xl, xh, yl, yh):
    around = neighbours(field, *sides_of((xl, xh, yl, yh)), 8)
    total = faces_ref[0] * around[0]
    for i in range(1, 6):
        total += faces_ref[i] * around[i]
    return total


def tile_second(now_ref, sums_ref, faces_ref, yh, xh, yl, xl, after, next_ref, a, b, c, d):
    inflow = flow_in(now_ref[...], faces_ref, xl, xh, yl, yh)
    later = (sums_ref[2] + inflow) * sums_ref[0]
    next_ref[...] = later
    put_faces(later, (a, b, c, d))


def tile_scatter_again(recv_ref, cells_ref, sums_ref, split):
    turned = load_slots(recv_ref, 0, 1)
    put_split(split, 0, turned[:PAD_RANKS])
    put_split(split, 1, turned[PAD_RANKS : 2 * PAD_RANKS])
    scatter_cells(split, 2, cells_ref, sums_ref)


def tile_third(hits_ref, now_ref, sums_ref, faces_ref, cells_ref, yh, xh, yl, xl,
               out_ref, next_ref, last_ref, a, b, c, d, found):
    now = now_ref[...]
    inflow = flow_in(now, faces_ref, xl, xh, yl, yh)
    later = (sums_ref[1] + inflow + hits_ref[0]) * sums_ref[0]
    next_ref[...] = later
    put_faces(later, (a, b, c, d))
    last_ref[...] = sums_ref[1] + hits_ref[1] + now * sums_ref[3]
    found[...] = jnp.zeros_like(found)
    gather_cells([now, later], cells_ref, found)
    store_slots(out_ref, found[...], 0, 1)


def tile_last(now_ref, last_ref, sums_ref, faces_ref, yh, xh, yl, xl, after, out_ref):
    inflow = flow_in(now_ref[...], faces_ref, xl, xh, yl, yh)
    out_ref[...] = (last_ref[...] + inflow) * sums_ref[0]


def trade(block, axis, first):
    count = lax.axis_size(axis)
    if count == 1:
        return block
    way = lambda i: 1 if (i % 2 == 0) == first else -1
    return lax.ppermute(block, axis, [(i, (i + way(i)) % count) for i in range(count)])


def swap(faces):
    y_first = trade(faces[2], "cross", True)
    y_second = trade(faces[3], "cross", False)
    x_first = trade(faces[0], "flow", True)
    x_second = trade(faces[1], "flow", False)
    return y_second, x_second, y_first, x_first


def deliver(payload):
    return lax.all_to_all(payload, ("flow", "cross"), split_axis=0, concat_axis=0, tiled=True)


def on_device(
    matrix_start, storage, perm, frac_start, frac_store, frac_cond,
    segment_ids, block_counts, hit_tile, hit_cell, hit_weight,
):
    blocks = frac_start.shape[0]
    nx, ny, nz = matrix_start.shape
    rows = nx * ny
    start, storage, perm = [a.reshape(rows, nz) for a in (matrix_start, storage, perm)]
    field = shape(rows, nz)
    faces_of = lambda n: (shape(n * ny, nz), shape(n * ny, nz), shape(n * nx, nz), shape(n * nx, nz))
    owned = lambda dtype: pltpu.VMEM((blocks, LANES), dtype)

    hits, coef, slots = call(
        owner_first,
        (shape(512, 128), shape(5, blocks, LANES), shape(2, blocks, LANES, dtype=I32)),
        8,
        scratch=[
            owned(F32), owned(F32), owned(F32), owned(I32),
            pltpu.VMEM((2 * blocks, 128), I32), owned(I32), owned(F32),
            pltpu.SemaphoreType.DMA((7,)),
            pltpu.VMEM((10, blocks, LANES), F32),
        ],
        smem=(0,),
        remote=range(1, 8),
        microseconds=6,
        vmem=64 * 1024 * 1024 - 4096,
    )(
        block_counts, frac_start, frac_store, frac_cond, segment_ids,
        hit_tile.reshape(2 * blocks, 128), hit_cell, hit_weight,
    )
    hits = deliver(hits)
    around = swap(call(rock_faces, faces_of(2), 2)(perm, start))
    sums, cells = call(
        tile_scatter,
        (shape(4, rows, nz), shape(2, PAD_RANKS, LANES, dtype=I32)),
        1,
        scratch=[pltpu.VMEM((8, PAD_RANKS, LANES), F32)],
        microseconds=4,
    )(hits)
    found = pltpu.VMEM((2 * PAD_RANKS, LANES), F32)
    seen, first, sums, faces, *sides = call(
        tile_first,
        (shape(256, 128), field, shape(4, rows, nz), shape(6, rows, nz)) + faces_of(1),
        9,
        scratch=[found],
        microseconds=4,
    )(sums, cells, perm, start, storage, *around)
    seen = deliver(seen)
    around = swap(sides)

    pushed, partial = call(
        owner_middle,
        (shape(256, 128), shape(blocks, LANES)),
        8,
        remote=range(4, 8),
        scratch=[
            pltpu.VMEM((blocks, LANES, LANES), BF16),
            pltpu.VMEM((2, blocks, LANES), F32),
            pltpu.VMEM((4, blocks, LANES), F32),
        ],
        microseconds=5,
    )(seen, frac_start, coef, slots, *around)
    pushed = deliver(pushed)
    second, *sides = call(tile_second, (field,) + faces_of(1), 8, remote=(7,))(
        first, sums, faces, *around, partial
    )
    around = swap(sides)

    hits = call(
        tile_scatter_again,
        shape(2, rows, nz),
        2,
        scratch=[pltpu.VMEM((4, PAD_RANKS, LANES), F32)],
        microseconds=3,
    )(pushed, cells)
    seen, third, last, *sides = call(
        tile_third,
        (shape(256, 128), field, field) + faces_of(1),
        9,
        scratch=[found],
        microseconds=4,
    )(hits, second, sums, faces, cells, *around)
    seen = deliver(seen)
    around = swap(sides)
    frac, token = call(
        owner_last,
        (shape(blocks, LANES), shape(8, 128)),
        4,
        scratch=[pltpu.VMEM((2, blocks, LANES), F32)],
        microseconds=4,
    )(seen, coef, slots, partial)
    fourth = call(tile_last, field, 9)(third, last, sums, faces, *around, token)
    return fourth.reshape(nx, ny, nz), frac


def solution(mesh):
    grid = P("flow", "cross", None)
    owner = P(("flow", "cross"), None)
    counts, tiles = P(("flow", "cross")), P(("flow", "cross"), None, None)
    in_specs = (grid,) * 3 + (owner,) * 4 + (counts, tiles, owner, owner)
    return jax.shard_map(
        on_device, mesh=mesh, in_specs=in_specs, out_specs=(grid, owner), check_vma=False
    )
```

```python
import jax
import jax.numpy as jnp
from jax import lax
from jax.experimental import pallas as pl
from jax.experimental.pallas import tpu as pltpu
from jax.sharding import PartitionSpec as P

F32 = jnp.float32
BF16 = jnp.bfloat16
I32 = jnp.int32
I16 = jnp.int16

LANES = 256
HALF_RANKS = 36
PAD_RANKS = 40
ROWS = 64
VMEM_LIMIT = 40 * 1024 * 1024

NN = (((1,), (0,)), ((), ()))
NT = (((1,), (1,)), ((), ()))


def call(body, out_shape, n_in, scratch=(), smem=(), remote=(), microseconds=1, vmem=VMEM_LIMIT):
    def place(i):
        if i in smem:
            return pltpu.SMEM
        return pltpu.HBM if i in remote else pltpu.VMEM

    out_specs = jax.tree.map(lambda _: pl.BlockSpec(memory_space=pltpu.VMEM), out_shape)
    return pl.pallas_call(
        body,
        out_shape=out_shape,
        in_specs=[pl.BlockSpec(memory_space=place(i)) for i in range(n_in)],
        out_specs=out_specs,
        scratch_shapes=list(scratch),
        compiler_params=pltpu.CompilerParams(vmem_limit_bytes=vmem),
        cost_estimate=pl.CostEstimate(
            flops=0, bytes_accessed=int(microseconds * 3_000_000), transcendentals=0
        ),
    )


def shape(*dims, dtype=F32):
    return jax.ShapeDtypeStruct(dims, dtype)


def halves(value):
    high = value.astype(BF16).astype(F32)
    return high, value - high


def hot_rows(index_row, count):
    place = lax.broadcasted_iota(I16, (16, LANES), 0)
    index = jnp.broadcast_to(index_row, (16, LANES)).astype(I16)
    one, none = jnp.ones((16, LANES), BF16), jnp.zeros((16, LANES), BF16)
    return jnp.concatenate(
        [jnp.where(place == index - jnp.int16(16 * j), one, none) for j in range(count // 16)], axis=0
    )


def same(index_row, count):
    return lax.broadcasted_iota(I32, (count, LANES), 0) == index_row


def shift_right(x):
    return pltpu.roll(x, 1, 1)


def shift_left(x):
    return pltpu.roll(x, LANES - 1, 1)


def store_slots(out_ref, by_slot, group, groups):
    rows = by_slot.shape[0]
    if rows < 128:
        by_slot = jnp.concatenate([by_slot, jnp.zeros((128 - rows, LANES), F32)], axis=0)
    turned = by_slot.T
    for part in range(2):
        out_ref[pl.ds(group * 2 + part, 128, stride=2 * groups), :] = turned[
            part * 128 : part * 128 + 128
        ]


def load_slots(in_ref, group, groups):
    parts = [in_ref[pl.ds(group * 2 + part, 128, stride=2 * groups), :] for part in range(2)]
    return jnp.concatenate(parts, axis=0).T


def spread_ranks(split, b, rank_half):
    mine = same(rank_half, PAD_RANKS)
    rows = [jnp.where(mine, split[v, b : b + 1, :], 0.0) for v in range(split.shape[0])]
    return jnp.concatenate(rows, axis=0).astype(BF16)


def joined(total, height, count):
    return [
        total[2 * v * height : (2 * v + 1) * height] + total[(2 * v + 1) * height : (2 * v + 2) * height]
        for v in range(count)
    ]


def put_split(split, v, value):
    high, low = halves(value)
    split[2 * v] = high
    split[2 * v + 1] = low


def owner_first(
    count_ref, start_hbm, store_hbm, cond_hbm, seg_hbm, tile_hbm, cell_hbm, weight_hbm,
    out_ref, coef_ref, slot_ref,
    start_ref, store_ref, cond_ref, seg_ref, tile_ref, cell_ref, weight_ref, arrived, split,
):
    pairs = [
        (tile_hbm, tile_ref), (seg_hbm, seg_ref), (cond_hbm, cond_ref), (weight_hbm, weight_ref),
        (store_hbm, store_ref), (start_hbm, start_ref), (cell_hbm, cell_ref),
    ]
    copies = [pltpu.make_async_copy(a, b, arrived.at[i]) for i, (a, b) in enumerate(pairs)]
    for copy in copies:
        copy.start()
    for copy in copies:
        copy.wait()
    blocks = start_ref.shape[0]
    size = (blocks, LANES)
    live = lax.broadcasted_iota(I32, size, 0) < count_ref[0]
    lane = lax.broadcasted_iota(I32, size, 1)
    start = start_ref[...]
    store = store_ref[...]
    weight = jnp.where(live, weight_ref[...], 0.0)
    seg = seg_ref[...]
    linked = (seg == shift_left(seg)) & (lane < LANES - 1)
    right = jnp.where(linked, cond_ref[...], 0.0)
    left = shift_right(right)
    inverse = 1.0 / (store + left + right + weight)
    own = jnp.where(live, store * start * inverse, start)
    left = jnp.where(live, left * inverse, 0.0)
    right = jnp.where(live, right * inverse, 0.0)
    pull = weight * inverse
    coef_ref[0] = own
    coef_ref[1] = left
    coef_ref[2] = right
    coef_ref[3] = pull
    coef_ref[4] = weight
    partial = own + left * shift_right(start) + right * shift_left(start)
    put_split(split, 0, cell_ref[...].astype(F32))
    put_split(split, 1, weight)
    put_split(split, 2, weight * start)
    put_split(split, 3, weight * partial)
    put_split(split, 4, weight * pull)
    tile = jnp.concatenate(
        [tile_ref[pl.ds(0, blocks, stride=2), :], tile_ref[pl.ds(1, blocks, stride=2), :]], axis=1
    )
    slot_ref[0] = jnp.where(live, tile, -1)
    upper = jnp.where(
        lax.broadcasted_iota(I32, (LANES, LANES), 0) <= lax.broadcasted_iota(I32, (LANES, LANES), 1),
        1.0, 0.0,
    ).astype(BF16)
    before = jnp.zeros((128, LANES), F32)
    for b in range(blocks):
        target = slot_ref[0, b : b + 1, :]
        mine = same(target, 128)
        running = lax.dot_general(
            jnp.where(mine, 1.0, 0.0).astype(BF16), upper, NN, preferred_element_type=F32
        )
        rank = jnp.sum(jnp.where(mine, running + before, 0.0), axis=0, keepdims=True).astype(I32) - 1
        before += jnp.broadcast_to(running[:, LANES - 1 :], (128, LANES))
        slot_ref[1, b : b + 1, :] = jnp.maximum(rank, 0)
    target, rank = slot_ref[0], slot_ref[1]
    slot_ref[0] = jnp.where(live, target + (rank & 1) * 128, -1)
    slot_ref[1] = rank >> 1
    total = jnp.zeros((10 * PAD_RANKS, LANES), F32)
    for b in range(blocks):
        total += lax.dot_general(
            spread_ranks(split, b, slot_ref[1, b : b + 1, :]),
            hot_rows(slot_ref[0, b : b + 1, :], LANES), NT, preferred_element_type=F32,
        )
    sums = joined(total, PAD_RANKS, 5)
    store_slots(out_ref, jnp.concatenate(sums[:3], axis=0), 0, 2)
    store_slots(out_ref, jnp.concatenate(sums[3:], axis=0), 1, 2)


def unpack(recv_ref, slot_ref, key_hot, seen, blocks):
    turned = load_slots(recv_ref, 0, 1)[: 2 * PAD_RANKS]
    table = jnp.concatenate(halves(turned), axis=0).astype(BF16)
    for b in range(blocks):
        hot = hot_rows(slot_ref[0, b : b + 1, :], LANES)
        if key_hot is not None:
            key_hot[b] = hot
        found = lax.dot_general(table, hot, NN, preferred_element_type=F32)
        found = found[: 2 * PAD_RANKS] + found[2 * PAD_RANKS :]
        mine = same(slot_ref[1, b : b + 1, :], PAD_RANKS)
        for v in range(2):
            part = jnp.where(mine, found[v * PAD_RANKS : (v + 1) * PAD_RANKS], 0.0)
            seen[v, b : b + 1, :] = jnp.sum(part, axis=0, keepdims=True)


def owner_middle(
    recv_ref, start_ref, coef_ref, slot_ref, x_b, x_a, out_ref, partial_ref, key_hot, seen, split
):
    blocks = start_ref.shape[0]
    unpack(recv_ref, slot_ref, key_hot, seen, blocks)
    own, left, right, pull, weight = [coef_ref[i] for i in range(5)]
    now = start_ref[...]
    for v in range(2):
        now = own + left * shift_right(now) + right * shift_left(now) + pull * seen[v]
    partial = own + left * shift_right(now) + right * shift_left(now)
    partial_ref[...] = partial
    put_split(split, 0, weight * now)
    put_split(split, 1, weight * partial)
    total = jnp.zeros((4 * PAD_RANKS, LANES), F32)
    for b in range(blocks):
        total += lax.dot_general(
            spread_ranks(split, b, slot_ref[1, b : b + 1, :]), key_hot[b], NT,
            preferred_element_type=F32,
        )
    store_slots(out_ref, jnp.concatenate(joined(total, PAD_RANKS, 2), axis=0), 0, 1)


def owner_last(recv_ref, coef_ref, slot_ref, partial_ref, out_ref, token_ref, seen):
    token_ref[...] = jnp.zeros_like(token_ref)
    blocks = partial_ref.shape[0]
    unpack(recv_ref, slot_ref, None, seen, blocks)
    own, left, right, pull = [coef_ref[i] for i in range(4)]
    now = partial_ref[...] + pull * seen[0]
    out_ref[...] = own + left * shift_right(now) + right * shift_left(now) + pull * seen[1]


def fold(field):
    return jnp.concatenate([field[:, :LANES], field[:, LANES:]], axis=0)


def unfold(rows):
    half = ROWS // 2
    return jnp.concatenate([rows[:half], rows[half:]], axis=1)


def gather_cells(fields, cell_ref, found_ref):
    parts = []
    for field in fields:
        parts += halves(fold(field))
    table = jnp.concatenate(parts, axis=0).astype(BF16)
    for r in range(HALF_RANKS):
        mine = same(cell_ref[0, r : r + 1, :], ROWS)
        hot = hot_rows(cell_ref[1, r : r + 1, :], LANES)
        found = lax.dot_general(table, hot, NN, preferred_element_type=F32)
        for v, both in enumerate(joined(found, ROWS, len(fields))):
            found_ref[v * PAD_RANKS + r : v * PAD_RANKS + r + 1, :] = jnp.sum(
                jnp.where(mine, both, 0.0), axis=0, keepdims=True
            )


def scatter_cells(split, count, cell_ref, sums_ref):
    place = lax.broadcasted_iota(I16, (16, LANES), 0)
    none = jnp.zeros((16, LANES), BF16)
    total = jnp.zeros((2 * count * ROWS, LANES), F32)
    for r in range(HALF_RANKS):
        row = jnp.broadcast_to(cell_ref[0, r : r + 1, :], (16, LANES)).astype(I16)
        mine = [place == row - jnp.int16(16 * j) for j in range(ROWS // 16)]
        rows = []
        for v in range(2 * count):
            value = jnp.broadcast_to(split[v, r : r + 1, :], (16, LANES)).astype(BF16)
            rows += [jnp.where(m, value, none) for m in mine]
        hot = hot_rows(cell_ref[1, r : r + 1, :], LANES)
        total += lax.dot_general(
            jnp.concatenate(rows, axis=0), hot, NT, preferred_element_type=F32
        )
    for v, both in enumerate(joined(total, ROWS, count)):
        sums_ref[v] = unfold(both)


def pick(odd, yes, no):
    return jnp.where(odd, yes, no)


def parity():
    return lax.axis_index("flow") % 2 == 1, lax.axis_index("cross") % 2 == 1


def y_layer(field, y):
    return jnp.concatenate([field[i + y : i + y + 1] for i in range(0, field.shape[0], 8)], axis=0)


def widen(layer):
    rows, nz = layer.shape
    return jnp.concatenate(
        [jnp.broadcast_to(layer[i : i + 1], (8, nz)) for i in range(rows)], axis=0
    )


def put_faces(field, refs, place=0):
    rows = field.shape[0]
    odd_x, odd_y = parity()
    x_low, x_high = field[:8], field[rows - 8 :]
    y_low, y_high = y_layer(field, 0), y_layer(field, 7)
    at_x, at_y = pl.ds(place * 8, 8), pl.ds(place * (rows // 8), rows // 8)
    refs[0][at_x, :] = pick(odd_x, x_low, x_high)
    refs[1][at_x, :] = pick(odd_x, x_high, x_low)
    refs[2][at_y, :] = pick(odd_y, y_low, y_high)
    refs[3][at_y, :] = pick(odd_y, y_high, y_low)


def sides_of(refs, place=0, rows=32):
    odd_x, odd_y = parity()
    at_x, at_y = pl.ds(place * 8, 8), pl.ds(place * (rows // 8), rows // 8)
    x_first, x_second = refs[0][at_x, :], refs[1][at_x, :]
    y_first, y_second = refs[2][at_y, :], refs[3][at_y, :]
    return (
        pick(odd_x, x_first, x_second),
        pick(odd_x, x_second, x_first),
        pick(odd_y, y_first, y_second),
        pick(odd_y, y_second, y_first),
    )


def rock_faces(perm_ref, start_ref, *sides):
    put_faces(perm_ref[...], sides, 0)
    put_faces(start_ref[...], sides, 1)


def neighbours(field, x_low, x_high, y_low, y_high, ny):
    rows, nz = field.shape
    nx = rows // ny
    west = jnp.concatenate([x_low, field[: rows - ny]], axis=0)
    east = jnp.concatenate([field[ny:], x_high], axis=0)
    place = lax.broadcasted_iota(I32, (rows, nz), 0) % ny
    wide_low = jnp.concatenate(
        [jnp.broadcast_to(y_low[i : i + 1], (ny, nz)) for i in range(nx)], axis=0
    )
    wide_high = jnp.concatenate(
        [jnp.broadcast_to(y_high[i : i + 1], (ny, nz)) for i in range(nx)], axis=0
    )
    south = jnp.where(place == 0, wide_low, pltpu.roll(field, 1, 0))
    north = jnp.where(place == ny - 1, wide_high, pltpu.roll(field, rows - 1, 0))
    below = pltpu.roll(field, 1, 1)
    above = pltpu.roll(field, nz - 1, 1)
    return west, east, south, north, below, above


def tile_scatter(recv_ref, sums_ref, cells_ref, split):
    first = load_slots(recv_ref, 0, 2)
    second = load_slots(recv_ref, 1, 2)
    cell = first[:PAD_RANKS].astype(I32)
    deep = cell & 511
    cells_ref[0] = ((deep >> 8) << 5) + (cell >> 9)
    cells_ref[1] = deep & (LANES - 1)
    put_split(split, 0, first[PAD_RANKS : 2 * PAD_RANKS])
    put_split(split, 1, first[2 * PAD_RANKS : 3 * PAD_RANKS])
    put_split(split, 2, second[:PAD_RANKS])
    put_split(split, 3, second[PAD_RANKS : 2 * PAD_RANKS])
    scatter_cells(split, 4, cells_ref, sums_ref)


def tile_first(hits_ref, cells_ref, perm_ref, start_ref, storage_ref, yh, xh, yl, xl,
               out_ref, next_ref, sums_ref, faces_ref, known_ref, x_a, x_b, found):
    rows, nz = perm_ref.shape
    ny = 8
    perm = perm_ref[...]
    start = start_ref[...]
    beside = neighbours(perm, *sides_of((xl, xh, yl, yh), 0), ny)
    around = neighbours(start, *sides_of((xl, xh, yl, yh), 1), ny)
    i_flow, i_cross = lax.axis_index("flow"), lax.axis_index("cross")
    row = lax.broadcasted_iota(I32, (rows, nz), 0)
    lane = lax.broadcasted_iota(I32, (rows, nz), 1)
    closed = [
        (row < ny) & (i_flow == 0),
        (row >= rows - ny) & (i_flow == lax.axis_size("flow") - 1),
        (row % ny == 0) & (i_cross == 0),
        (row % ny == ny - 1) & (i_cross == lax.axis_size("cross") - 1),
        lane == 0,
        lane == nz - 1,
    ]
    storage = storage_ref[...]
    base = storage * start
    inflow = jnp.zeros_like(start)
    total = storage + hits_ref[0]
    for i in range(6):
        face = jnp.where(closed[i], 0.0, 2.0 * perm * beside[i] / (perm + beside[i]))
        faces_ref[i] = face
        total += face
        inflow += face * around[i]
    inverse = 1.0 / total
    now = (base + inflow + hits_ref[1]) * inverse
    next_ref[...] = now
    sums_ref[0] = inverse
    sums_ref[1] = base
    sums_ref[2] = hits_ref[3]
    far, near = jnp.zeros((ny, nz), F32), jnp.zeros((rows // ny, nz), F32)
    within = neighbours(now, far, far, near, near, ny)
    inflow = base + hits_ref[2] + start * hits_ref[3]
    for i in range(6):
        inflow += faces_ref[i] * within[i]
    known = inflow * inverse
    known_ref[...] = known
    south, north = faces_ref[2] * inverse, faces_ref[3] * inverse
    spare = jnp.zeros((6, nz), F32)
    odd_x, _ = parity()
    sides = []
    for x, face in ((0, 0), (rows // ny - 1, 1)):
        at, end = x * ny, x * ny + ny
        layers = [a[at:end] for a in (now, known, faces_ref[face] * inverse)]
        sides.append(
            jnp.concatenate(layers + [south[at : at + 1], north[end - 1 : end], spare], axis=0)
        )
    x_a[...] = pick(odd_x, sides[0], sides[1])
    x_b[...] = pick(odd_x, sides[1], sides[0])
    found[...] = jnp.zeros_like(found)
    gather_cells([start, now], cells_ref, found)
    store_slots(out_ref, found[...], 0, 1)


def flow_in(field, faces_ref, xl, xh, yl, yh):
    around = neighbours(field, *sides_of((xl, xh, yl, yh)), 8)
    total = faces_ref[0] * around[0]
    for i in range(1, 6):
        total += faces_ref[i] * around[i]
    return total


def tile_second(known_ref, now_ref, sums_ref, faces_ref, x_b, x_a, after, next_ref, y_a, y_b):
    odd_x, odd_y = parity()
    x_low, x_high = pick(odd_x, x_a[...], x_b[...]), pick(odd_x, x_b[...], x_a[...])
    now, inverse = now_ref[...], sums_ref[0]
    rows, nz = now.shape
    idle = jnp.zeros((rows - 16, nz), F32)
    west, east = faces_ref[0] * inverse, faces_ref[1] * inverse
    later = known_ref[...] + jnp.concatenate(
        [west[:8] * x_low[:8], idle, east[rows - 8 :] * x_high[:8]], axis=0
    )
    next_ref[...] = later
    spare = jnp.zeros((2, nz), F32)
    sides = []
    for y, face in ((0, 2), (7, 3)):
        layers = [y_layer(a, y) for a in (now, later, faces_ref[face] * inverse)]
        corners = [x_low[y : y + 1], x_high[y : y + 1]]
        sides.append(jnp.concatenate(layers + corners + [spare], axis=0))
    y_a[...] = pick(odd_y, sides[0], sides[1])
    y_b[...] = pick(odd_y, sides[1], sides[0])


def tile_scatter_again(recv_ref, cells_ref, sums_ref, split):
    turned = load_slots(recv_ref, 0, 1)
    put_split(split, 0, turned[:PAD_RANKS])
    put_split(split, 1, turned[PAD_RANKS : 2 * PAD_RANKS])
    scatter_cells(split, 2, cells_ref, sums_ref)


def tile_third(hits_ref, part_ref, before_ref, sums_ref, faces_ref, cells_ref, y_b, y_a, x_b, x_a,
               out_ref, next_ref, last_ref, a, b, c, d, found):
    odd_x, odd_y = parity()
    x_low, x_high = pick(odd_x, x_a[...], x_b[...]), pick(odd_x, x_b[...], x_a[...])
    y_low, y_high = pick(odd_y, y_a[...], y_b[...]), pick(odd_y, y_b[...], y_a[...])
    before, inverse = before_ref[...], sums_ref[0]
    rows, nz = before.shape
    nx = rows // 8
    y = lax.broadcasted_iota(I32, (rows, nz), 0) % 8
    inflow = jnp.where(y == 0, faces_ref[2] * widen(y_low[:nx]), 0.0)
    inflow += jnp.where(y == 7, faces_ref[3] * widen(y_high[:nx]), 0.0)
    now = part_ref[...] + inflow * inverse
    sides = []
    still = jnp.zeros((6, nz), F32)
    for i, (side, at) in enumerate(((x_low, 0), (x_high, rows - 8))):
        corner = slice(3 * nx + i, 3 * nx + i + 1)
        corners = [side[24:25] * y_low[corner], still, side[25:26] * y_high[corner]]
        sides.append(
            side[8:16] + side[16:24] * before[at : at + 8] + jnp.concatenate(corners, axis=0)
        )
    for side, at in ((y_low, 0), (y_high, 7)):
        sides.append(side[nx : 2 * nx] + side[2 * nx : 3 * nx] * y_layer(before, at))
    around = neighbours(now, *sides, 8)
    inflow = sums_ref[1] + hits_ref[0]
    for i in range(6):
        inflow += faces_ref[i] * around[i]
    later = inflow * inverse
    next_ref[...] = later
    put_faces(later, (a, b, c, d))
    last_ref[...] = sums_ref[1] + hits_ref[1] + now * sums_ref[2]
    found[...] = jnp.zeros_like(found)
    gather_cells([now, later], cells_ref, found)
    store_slots(out_ref, found[...], 0, 1)


def tile_last(now_ref, last_ref, sums_ref, faces_ref, yh, xh, yl, xl, after, out_ref):
    inflow = flow_in(now_ref[...], faces_ref, xl, xh, yl, yh)
    out_ref[...] = (last_ref[...] + inflow) * sums_ref[0]


def trade(block, axis, first):
    count = lax.axis_size(axis)
    if count == 1:
        return block
    way = lambda i: 1 if (i % 2 == 0) == first else -1
    return lax.ppermute(block, axis, [(i, (i + way(i)) % count) for i in range(count)])


def swap(faces):
    y_first = trade(faces[2], "cross", True)
    y_second = trade(faces[3], "cross", False)
    x_first = trade(faces[0], "flow", True)
    x_second = trade(faces[1], "flow", False)
    return y_second, x_second, y_first, x_first


def deliver(payload):
    return lax.all_to_all(payload, ("flow", "cross"), split_axis=0, concat_axis=0, tiled=True)


def on_device(
    matrix_start, storage, perm, frac_start, frac_store, frac_cond,
    segment_ids, block_counts, hit_tile, hit_cell, hit_weight,
):
    blocks = frac_start.shape[0]
    nx, ny, nz = matrix_start.shape
    rows = nx * ny
    start, storage, perm = [a.reshape(rows, nz) for a in (matrix_start, storage, perm)]
    field = shape(rows, nz)
    faces_of = lambda n: (shape(n * ny, nz), shape(n * ny, nz), shape(n * nx, nz), shape(n * nx, nz))
    owned = lambda dtype: pltpu.VMEM((blocks, LANES), dtype)

    hits, coef, slots = call(
        owner_first,
        (shape(512, 128), shape(5, blocks, LANES), shape(2, blocks, LANES, dtype=I32)),
        8,
        scratch=[
            owned(F32), owned(F32), owned(F32), owned(I32),
            pltpu.VMEM((2 * blocks, 128), I32), owned(I32), owned(F32),
            pltpu.SemaphoreType.DMA((7,)),
            pltpu.VMEM((10, blocks, LANES), F32),
        ],
        smem=(0,),
        remote=range(1, 8),
        microseconds=6,
        vmem=64 * 1024 * 1024 - 4096,
    )(
        block_counts, frac_start, frac_store, frac_cond, segment_ids,
        hit_tile.reshape(2 * blocks, 128), hit_cell, hit_weight,
    )
    hits = deliver(hits)
    around = swap(call(rock_faces, faces_of(2), 2)(perm, start))
    sums, cells = call(
        tile_scatter,
        (shape(4, rows, nz), shape(2, PAD_RANKS, LANES, dtype=I32)),
        1,
        scratch=[pltpu.VMEM((8, PAD_RANKS, LANES), F32)],
        microseconds=4,
    )(hits)
    found = pltpu.VMEM((2 * PAD_RANKS, LANES), F32)
    y_side, x_side = shape(4 * nx, nz), shape(4 * ny, nz)
    seen, first, sums, faces, known, x_a, x_b = call(
        tile_first,
        (shape(256, 128), field, shape(3, rows, nz), shape(6, rows, nz), field, x_side, x_side),
        9,
        scratch=[found],
        microseconds=4,
    )(sums, cells, perm, start, storage, *around)
    seen = deliver(seen)
    beside_x = trade(x_b, "flow", False), trade(x_a, "flow", True)

    pushed, partial = call(
        owner_middle,
        (shape(256, 128), shape(blocks, LANES)),
        6,
        remote=(4, 5),
        scratch=[
            pltpu.VMEM((blocks, LANES, LANES), BF16),
            pltpu.VMEM((2, blocks, LANES), F32),
            pltpu.VMEM((4, blocks, LANES), F32),
        ],
        microseconds=5,
    )(seen, frac_start, coef, slots, *beside_x)
    pushed = deliver(pushed)
    second, y_a, y_b = call(tile_second, (field, y_side, y_side), 7, remote=(6,))(
        known, first, sums, faces, *beside_x, partial
    )
    beside_y = trade(y_b, "cross", False), trade(y_a, "cross", True)

    hits = call(
        tile_scatter_again,
        shape(2, rows, nz),
        2,
        scratch=[pltpu.VMEM((4, PAD_RANKS, LANES), F32)],
        microseconds=3,
    )(pushed, cells)
    seen, third, last, *sides = call(
        tile_third,
        (shape(256, 128), field, field) + faces_of(1),
        10,
        scratch=[found],
        microseconds=4,
    )(hits, second, first, sums, faces, cells, *beside_y, *beside_x)
    seen = deliver(seen)
    around = swap(sides)
    frac, token = call(
        owner_last,
        (shape(blocks, LANES), shape(8, 128)),
        4,
        scratch=[pltpu.VMEM((2, blocks, LANES), F32)],
        microseconds=4,
    )(seen, coef, slots, partial)
    fourth = call(tile_last, field, 9)(third, last, sums, faces, *around, token)
    return fourth.reshape(nx, ny, nz), frac


def solution(mesh):
    grid = P("flow", "cross", None)
    owner = P(("flow", "cross"), None)
    counts, tiles = P(("flow", "cross")), P(("flow", "cross"), None, None)
    in_specs = (grid,) * 3 + (owner,) * 4 + (counts, tiles, owner, owner)
    return jax.shard_map(
        on_device, mesh=mesh, in_specs=in_specs, out_specs=(grid, owner), check_vma=False
    )
```

```python
import jax
import jax.numpy as jnp
from jax import lax
from jax.experimental import pallas as pl
from jax.experimental.pallas import tpu as pltpu
from jax.sharding import PartitionSpec as P

F32 = jnp.float32
BF16 = jnp.bfloat16
I32 = jnp.int32
I16 = jnp.int16

LANES = 256
HALF_RANKS = 36
PAD_RANKS = 40
ROWS = 64
VMEM_LIMIT = 40 * 1024 * 1024

NN = (((1,), (0,)), ((), ()))
NT = (((1,), (1,)), ((), ()))


def call(body, out_shape, n_in, scratch=(), smem=(), remote=(), microseconds=1, vmem=VMEM_LIMIT):
    def place(i):
        if i in smem:
            return pltpu.SMEM
        return pltpu.HBM if i in remote else pltpu.VMEM

    out_specs = jax.tree.map(lambda _: pl.BlockSpec(memory_space=pltpu.VMEM), out_shape)
    return pl.pallas_call(
        body,
        out_shape=out_shape,
        in_specs=[pl.BlockSpec(memory_space=place(i)) for i in range(n_in)],
        out_specs=out_specs,
        scratch_shapes=list(scratch),
        compiler_params=pltpu.CompilerParams(vmem_limit_bytes=vmem),
        cost_estimate=pl.CostEstimate(
            flops=0, bytes_accessed=int(microseconds * 3_000_000), transcendentals=0
        ),
    )


def shape(*dims, dtype=F32):
    return jax.ShapeDtypeStruct(dims, dtype)


def halves(value):
    high = value.astype(BF16).astype(F32)
    return high, value - high


def hot_rows(index_row, count):
    place = lax.broadcasted_iota(I16, (16, LANES), 0)
    index = jnp.broadcast_to(index_row, (16, LANES)).astype(I16)
    one, none = jnp.ones((16, LANES), BF16), jnp.zeros((16, LANES), BF16)
    return jnp.concatenate(
        [jnp.where(place == index - jnp.int16(16 * j), one, none) for j in range(count // 16)], axis=0
    )


def same(index_row, count):
    return lax.broadcasted_iota(I32, (count, LANES), 0) == index_row


def shift_right(x):
    return pltpu.roll(x, 1, 1)


def shift_left(x):
    return pltpu.roll(x, LANES - 1, 1)


def store_slots(out_ref, by_slot, group, groups):
    rows = by_slot.shape[0]
    if rows < 128:
        by_slot = jnp.concatenate([by_slot, jnp.zeros((128 - rows, LANES), F32)], axis=0)
    turned = by_slot.T
    for part in range(2):
        out_ref[pl.ds(group * 2 + part, 128, stride=2 * groups), :] = turned[
            part * 128 : part * 128 + 128
        ]


def load_slots(in_ref, group, groups):
    parts = [in_ref[pl.ds(group * 2 + part, 128, stride=2 * groups), :] for part in range(2)]
    return jnp.concatenate(parts, axis=0).T


def spread_ranks(split, b, rank_half):
    mine = same(rank_half, PAD_RANKS)
    rows = [jnp.where(mine, split[v, b : b + 1, :], 0.0) for v in range(split.shape[0])]
    return jnp.concatenate(rows, axis=0).astype(BF16)


def joined(total, height, count):
    return [
        total[2 * v * height : (2 * v + 1) * height] + total[(2 * v + 1) * height : (2 * v + 2) * height]
        for v in range(count)
    ]


def put_split(split, v, value):
    high, low = halves(value)
    split[2 * v] = high
    split[2 * v + 1] = low


def owner_first(
    count_ref, start_hbm, store_hbm, cond_hbm, seg_hbm, tile_hbm, cell_hbm, weight_hbm,
    out_ref, coef_ref, slot_ref,
    start_ref, store_ref, cond_ref, seg_ref, tile_ref, cell_ref, weight_ref, arrived, split,
):
    pairs = [
        (tile_hbm, tile_ref), (seg_hbm, seg_ref), (cond_hbm, cond_ref), (weight_hbm, weight_ref),
        (store_hbm, store_ref), (start_hbm, start_ref), (cell_hbm, cell_ref),
    ]
    copies = [pltpu.make_async_copy(a, b, arrived.at[i]) for i, (a, b) in enumerate(pairs)]
    for copy in copies:
        copy.start()
    for copy in copies:
        copy.wait()
    blocks = start_ref.shape[0]
    size = (blocks, LANES)
    live = lax.broadcasted_iota(I32, size, 0) < count_ref[0]
    lane = lax.broadcasted_iota(I32, size, 1)
    start = start_ref[...]
    store = store_ref[...]
    weight = jnp.where(live, weight_ref[...], 0.0)
    seg = seg_ref[...]
    linked = (seg == shift_left(seg)) & (lane < LANES - 1)
    right = jnp.where(linked, cond_ref[...], 0.0)
    left = shift_right(right)
    inverse = 1.0 / (store + left + right + weight)
    own = jnp.where(live, store * start * inverse, start)
    left = jnp.where(live, left * inverse, 0.0)
    right = jnp.where(live, right * inverse, 0.0)
    pull = weight * inverse
    coef_ref[0] = own
    coef_ref[1] = left
    coef_ref[2] = right
    coef_ref[3] = pull
    coef_ref[4] = weight
    partial = own + left * shift_right(start) + right * shift_left(start)
    put_split(split, 0, cell_ref[...].astype(F32))
    put_split(split, 1, weight)
    put_split(split, 2, weight * start)
    put_split(split, 3, weight * partial)
    put_split(split, 4, weight * pull)
    tile = jnp.concatenate(
        [tile_ref[pl.ds(0, blocks, stride=2), :], tile_ref[pl.ds(1, blocks, stride=2), :]], axis=1
    )
    slot_ref[0] = jnp.where(live, tile, -1)
    upper = jnp.where(
        lax.broadcasted_iota(I32, (LANES, LANES), 0) <= lax.broadcasted_iota(I32, (LANES, LANES), 1),
        1.0, 0.0,
    ).astype(BF16)
    before = jnp.zeros((128, LANES), F32)
    for b in range(blocks):
        target = slot_ref[0, b : b + 1, :]
        mine = same(target, 128)
        running = lax.dot_general(
            jnp.where(mine, 1.0, 0.0).astype(BF16), upper, NN, preferred_element_type=F32
        )
        rank = jnp.sum(jnp.where(mine, running + before, 0.0), axis=0, keepdims=True).astype(I32) - 1
        before += jnp.broadcast_to(running[:, LANES - 1 :], (128, LANES))
        slot_ref[1, b : b + 1, :] = jnp.maximum(rank, 0)
    target, rank = slot_ref[0], slot_ref[1]
    slot_ref[0] = jnp.where(live, target + (rank & 1) * 128, -1)
    slot_ref[1] = rank >> 1
    total = jnp.zeros((10 * PAD_RANKS, LANES), F32)
    for b in range(blocks):
        total += lax.dot_general(
            spread_ranks(split, b, slot_ref[1, b : b + 1, :]),
            hot_rows(slot_ref[0, b : b + 1, :], LANES), NT, preferred_element_type=F32,
        )
    sums = joined(total, PAD_RANKS, 5)
    store_slots(out_ref, jnp.concatenate(sums[:3], axis=0), 0, 2)
    store_slots(out_ref, jnp.concatenate(sums[3:], axis=0), 1, 2)


def unpack(recv_ref, slot_ref, key_hot, seen, blocks):
    turned = load_slots(recv_ref, 0, 1)[: 2 * PAD_RANKS]
    table = jnp.concatenate(halves(turned), axis=0).astype(BF16)
    for b in range(blocks):
        hot = hot_rows(slot_ref[0, b : b + 1, :], LANES)
        if key_hot is not None:
            key_hot[b] = hot
        found = lax.dot_general(table, hot, NN, preferred_element_type=F32)
        found = found[: 2 * PAD_RANKS] + found[2 * PAD_RANKS :]
        mine = same(slot_ref[1, b : b + 1, :], PAD_RANKS)
        for v in range(2):
            part = jnp.where(mine, found[v * PAD_RANKS : (v + 1) * PAD_RANKS], 0.0)
            seen[v, b : b + 1, :] = jnp.sum(part, axis=0, keepdims=True)


def owner_middle(
    recv_ref, start_ref, coef_ref, slot_ref, x_b, x_a, out_ref, partial_ref, key_hot, seen, split
):
    blocks = start_ref.shape[0]
    unpack(recv_ref, slot_ref, key_hot, seen, blocks)
    own, left, right, pull, weight = [coef_ref[i] for i in range(5)]
    now = start_ref[...]
    for v in range(2):
        now = own + left * shift_right(now) + right * shift_left(now) + pull * seen[v]
    partial = own + left * shift_right(now) + right * shift_left(now)
    partial_ref[...] = partial
    put_split(split, 0, weight * now)
    put_split(split, 1, weight * partial)
    total = jnp.zeros((4 * PAD_RANKS, LANES), F32)
    for b in range(blocks):
        total += lax.dot_general(
            spread_ranks(split, b, slot_ref[1, b : b + 1, :]), key_hot[b], NT,
            preferred_element_type=F32,
        )
    store_slots(out_ref, jnp.concatenate(joined(total, PAD_RANKS, 2), axis=0), 0, 1)


def fold(field):
    return jnp.concatenate([field[:, :LANES], field[:, LANES:]], axis=0)


def unfold(rows):
    half = ROWS // 2
    return jnp.concatenate([rows[:half], rows[half:]], axis=1)


def gather_cells(fields, cell_ref, found_ref):
    parts = []
    for field in fields:
        parts += halves(fold(field))
    table = jnp.concatenate(parts, axis=0).astype(BF16)
    for r in range(HALF_RANKS):
        mine = same(cell_ref[0, r : r + 1, :], ROWS)
        hot = hot_rows(cell_ref[1, r : r + 1, :], LANES)
        found = lax.dot_general(table, hot, NN, preferred_element_type=F32)
        for v, both in enumerate(joined(found, ROWS, len(fields))):
            found_ref[v * PAD_RANKS + r : v * PAD_RANKS + r + 1, :] = jnp.sum(
                jnp.where(mine, both, 0.0), axis=0, keepdims=True
            )


def scatter_cells(split, count, cell_ref, sums_ref):
    place = lax.broadcasted_iota(I16, (16, LANES), 0)
    none = jnp.zeros((16, LANES), BF16)
    total = jnp.zeros((2 * count * ROWS, LANES), F32)
    for r in range(HALF_RANKS):
        row = jnp.broadcast_to(cell_ref[0, r : r + 1, :], (16, LANES)).astype(I16)
        mine = [place == row - jnp.int16(16 * j) for j in range(ROWS // 16)]
        rows = []
        for v in range(2 * count):
            value = jnp.broadcast_to(split[v, r : r + 1, :], (16, LANES)).astype(BF16)
            rows += [jnp.where(m, value, none) for m in mine]
        hot = hot_rows(cell_ref[1, r : r + 1, :], LANES)
        total += lax.dot_general(
            jnp.concatenate(rows, axis=0), hot, NT, preferred_element_type=F32
        )
    for v, both in enumerate(joined(total, ROWS, count)):
        sums_ref[v] = unfold(both)


def pick(odd, yes, no):
    return jnp.where(odd, yes, no)


def parity():
    return lax.axis_index("flow") % 2 == 1, lax.axis_index("cross") % 2 == 1


def y_layer(field, y):
    return jnp.concatenate([field[i + y : i + y + 1] for i in range(0, field.shape[0], 8)], axis=0)


def widen(layer):
    rows, nz = layer.shape
    return jnp.concatenate(
        [jnp.broadcast_to(layer[i : i + 1], (8, nz)) for i in range(rows)], axis=0
    )


def put_faces(field, refs, place=0):
    rows = field.shape[0]
    odd_x, odd_y = parity()
    x_low, x_high = field[:8], field[rows - 8 :]
    y_low, y_high = y_layer(field, 0), y_layer(field, 7)
    at_x, at_y = pl.ds(place * 8, 8), pl.ds(place * (rows // 8), rows // 8)
    refs[0][at_x, :] = pick(odd_x, x_low, x_high)
    refs[1][at_x, :] = pick(odd_x, x_high, x_low)
    refs[2][at_y, :] = pick(odd_y, y_low, y_high)
    refs[3][at_y, :] = pick(odd_y, y_high, y_low)
    for ref in refs[2:]:
        ref[ref.shape[0] - 8 :, :] = jnp.zeros((8, field.shape[1]), F32)


def sides_of(refs, place=0, rows=32):
    odd_x, odd_y = parity()
    at_x, at_y = pl.ds(place * 8, 8), pl.ds(place * (rows // 8), rows // 8)
    x_first, x_second = refs[0][at_x, :], refs[1][at_x, :]
    y_first, y_second = refs[2][at_y, :], refs[3][at_y, :]
    return (
        pick(odd_x, x_first, x_second),
        pick(odd_x, x_second, x_first),
        pick(odd_y, y_first, y_second),
        pick(odd_y, y_second, y_first),
    )


def rock_faces(perm_ref, start_ref, *sides):
    put_faces(perm_ref[...], sides, 0)
    put_faces(start_ref[...], sides, 1)


def neighbours(field, x_low, x_high, y_low, y_high, ny):
    rows, nz = field.shape
    nx = rows // ny
    west = jnp.concatenate([x_low, field[: rows - ny]], axis=0)
    east = jnp.concatenate([field[ny:], x_high], axis=0)
    place = lax.broadcasted_iota(I32, (rows, nz), 0) % ny
    wide_low = jnp.concatenate(
        [jnp.broadcast_to(y_low[i : i + 1], (ny, nz)) for i in range(nx)], axis=0
    )
    wide_high = jnp.concatenate(
        [jnp.broadcast_to(y_high[i : i + 1], (ny, nz)) for i in range(nx)], axis=0
    )
    south = jnp.where(place == 0, wide_low, pltpu.roll(field, 1, 0))
    north = jnp.where(place == ny - 1, wide_high, pltpu.roll(field, rows - 1, 0))
    below = pltpu.roll(field, 1, 1)
    above = pltpu.roll(field, nz - 1, 1)
    return west, east, south, north, below, above


def tile_scatter(recv_ref, sums_ref, cells_ref, split):
    first = load_slots(recv_ref, 0, 2)
    second = load_slots(recv_ref, 1, 2)
    cell = first[:PAD_RANKS].astype(I32)
    deep = cell & 511
    cells_ref[0] = ((deep >> 8) << 5) + (cell >> 9)
    cells_ref[1] = deep & (LANES - 1)
    put_split(split, 0, first[PAD_RANKS : 2 * PAD_RANKS])
    put_split(split, 1, first[2 * PAD_RANKS : 3 * PAD_RANKS])
    put_split(split, 2, second[:PAD_RANKS])
    put_split(split, 3, second[PAD_RANKS : 2 * PAD_RANKS])
    scatter_cells(split, 4, cells_ref, sums_ref)


def tile_first(hits_ref, cells_ref, perm_ref, start_ref, storage_ref, yh, xh, yl, xl,
               out_ref, next_ref, sums_ref, faces_ref, known_ref, x_a, x_b, found):
    rows, nz = perm_ref.shape
    ny = 8
    perm = perm_ref[...]
    start = start_ref[...]
    beside = neighbours(perm, *sides_of((xl, xh, yl, yh), 0), ny)
    around = neighbours(start, *sides_of((xl, xh, yl, yh), 1), ny)
    i_flow, i_cross = lax.axis_index("flow"), lax.axis_index("cross")
    row = lax.broadcasted_iota(I32, (rows, nz), 0)
    lane = lax.broadcasted_iota(I32, (rows, nz), 1)
    closed = [
        (row < ny) & (i_flow == 0),
        (row >= rows - ny) & (i_flow == lax.axis_size("flow") - 1),
        (row % ny == 0) & (i_cross == 0),
        (row % ny == ny - 1) & (i_cross == lax.axis_size("cross") - 1),
        lane == 0,
        lane == nz - 1,
    ]
    storage = storage_ref[...]
    base = storage * start
    inflow = jnp.zeros_like(start)
    total = storage + hits_ref[0]
    for i in range(6):
        face = jnp.where(closed[i], 0.0, 2.0 * perm * beside[i] / (perm + beside[i]))
        faces_ref[i] = face
        total += face
        inflow += face * around[i]
    inverse = 1.0 / total
    now = (base + inflow + hits_ref[1]) * inverse
    next_ref[...] = now
    sums_ref[0] = inverse
    sums_ref[1] = base
    sums_ref[2] = hits_ref[3]
    far, near = jnp.zeros((ny, nz), F32), jnp.zeros((rows // ny, nz), F32)
    within = neighbours(now, far, far, near, near, ny)
    inflow = base + hits_ref[2] + start * hits_ref[3]
    for i in range(6):
        inflow += faces_ref[i] * within[i]
    known = inflow * inverse
    known_ref[...] = known
    south, north = faces_ref[2] * inverse, faces_ref[3] * inverse
    spare = jnp.zeros((6, nz), F32)
    odd_x, _ = parity()
    sides = []
    for x, face in ((0, 0), (rows // ny - 1, 1)):
        at, end = x * ny, x * ny + ny
        layers = [a[at:end] for a in (now, known, faces_ref[face] * inverse)]
        sides.append(
            jnp.concatenate(layers + [south[at : at + 1], north[end - 1 : end], spare], axis=0)
        )
    x_a[...] = pick(odd_x, sides[0], sides[1])
    x_b[...] = pick(odd_x, sides[1], sides[0])
    found[...] = jnp.zeros_like(found)
    gather_cells([start, now], cells_ref, found)
    store_slots(out_ref, found[...], 0, 1)


def flow_in(field, faces_ref, xl, xh, yl, yh):
    around = neighbours(field, *sides_of((xl, xh, yl, yh)), 8)
    total = faces_ref[0] * around[0]
    for i in range(1, 6):
        total += faces_ref[i] * around[i]
    return total


def tile_second(known_ref, now_ref, sums_ref, faces_ref, x_b, x_a, after, next_ref, y_a, y_b):
    odd_x, odd_y = parity()
    x_low, x_high = pick(odd_x, x_a[...], x_b[...]), pick(odd_x, x_b[...], x_a[...])
    now, inverse = now_ref[...], sums_ref[0]
    rows, nz = now.shape
    idle = jnp.zeros((rows - 16, nz), F32)
    west, east = faces_ref[0] * inverse, faces_ref[1] * inverse
    later = known_ref[...] + jnp.concatenate(
        [west[:8] * x_low[:8], idle, east[rows - 8 :] * x_high[:8]], axis=0
    )
    next_ref[...] = later
    spare = jnp.zeros((2, nz), F32)
    sides = []
    for y, face in ((0, 2), (7, 3)):
        layers = [y_layer(a, y) for a in (now, later, faces_ref[face] * inverse)]
        corners = [x_low[y : y + 1], x_high[y : y + 1]]
        sides.append(jnp.concatenate(layers + corners + [spare], axis=0))
    y_a[...] = pick(odd_y, sides[0], sides[1])
    y_b[...] = pick(odd_y, sides[1], sides[0])


def tile_scatter_again(recv_ref, cells_ref, sums_ref, split):
    turned = load_slots(recv_ref, 0, 1)
    put_split(split, 0, turned[:PAD_RANKS])
    put_split(split, 1, turned[PAD_RANKS : 2 * PAD_RANKS])
    scatter_cells(split, 2, cells_ref, sums_ref)


def tile_third(hits_ref, part_ref, before_ref, sums_ref, faces_ref, cells_ref, y_b, y_a, x_b, x_a,
               out_ref, next_ref, last_ref, a, b, c, d, found):
    odd_x, odd_y = parity()
    x_low, x_high = pick(odd_x, x_a[...], x_b[...]), pick(odd_x, x_b[...], x_a[...])
    y_low, y_high = pick(odd_y, y_a[...], y_b[...]), pick(odd_y, y_b[...], y_a[...])
    before, inverse = before_ref[...], sums_ref[0]
    rows, nz = before.shape
    nx = rows // 8
    y = lax.broadcasted_iota(I32, (rows, nz), 0) % 8
    inflow = jnp.where(y == 0, faces_ref[2] * widen(y_low[:nx]), 0.0)
    inflow += jnp.where(y == 7, faces_ref[3] * widen(y_high[:nx]), 0.0)
    now = part_ref[...] + inflow * inverse
    sides = []
    still = jnp.zeros((6, nz), F32)
    for i, (side, at) in enumerate(((x_low, 0), (x_high, rows - 8))):
        corner = slice(3 * nx + i, 3 * nx + i + 1)
        corners = [side[24:25] * y_low[corner], still, side[25:26] * y_high[corner]]
        sides.append(
            side[8:16] + side[16:24] * before[at : at + 8] + jnp.concatenate(corners, axis=0)
        )
    for side, at in ((y_low, 0), (y_high, 7)):
        sides.append(side[nx : 2 * nx] + side[2 * nx : 3 * nx] * y_layer(before, at))
    around = neighbours(now, *sides, 8)
    inflow = sums_ref[1] + hits_ref[0]
    for i in range(6):
        inflow += faces_ref[i] * around[i]
    later = inflow * inverse
    next_ref[...] = later
    put_faces(later, (a, b, c, d))
    last_ref[...] = sums_ref[1] + hits_ref[1] + now * sums_ref[2]
    found[...] = jnp.zeros_like(found)
    gather_cells([now, later], cells_ref, found)
    store_slots(out_ref, found[...], 0, 1)


def last_pair(recv_ref, coef_ref, slot_ref, partial_ref, now_ref, last_ref, sums_ref, faces_ref,
              yh, xh, yl, xl, frac_ref, matrix_ref, seen):
    inflow = flow_in(now_ref[...], faces_ref, xl, xh, yl, yh)
    matrix_ref[...] = (last_ref[...] + inflow) * sums_ref[0]
    blocks = partial_ref.shape[0]
    unpack(recv_ref, slot_ref, None, seen, blocks)
    own, left, right, pull = [coef_ref[i] for i in range(4)]
    now = partial_ref[...] + pull * seen[0]
    frac_ref[...] = own + left * shift_right(now) + right * shift_left(now) + pull * seen[1]


def trade(block, axis, first):
    count = lax.axis_size(axis)
    if count == 1:
        return block
    way = lambda i: 1 if (i % 2 == 0) == first else -1
    return lax.ppermute(block, axis, [(i, (i + way(i)) % count) for i in range(count)])


def swap(faces):
    y_first = trade(faces[2], "cross", True)
    y_second = trade(faces[3], "cross", False)
    x_first = trade(faces[0], "flow", True)
    x_second = trade(faces[1], "flow", False)
    return y_second, x_second, y_first, x_first


def deliver(payload):
    return lax.all_to_all(payload, ("flow", "cross"), split_axis=0, concat_axis=0, tiled=True)


def on_device(
    matrix_start, storage, perm, frac_start, frac_store, frac_cond,
    segment_ids, block_counts, hit_tile, hit_cell, hit_weight,
):
    blocks = frac_start.shape[0]
    nx, ny, nz = matrix_start.shape
    rows = nx * ny
    start, storage, perm = [a.reshape(rows, nz) for a in (matrix_start, storage, perm)]
    field = shape(rows, nz)
    faces_of = lambda n: (shape(n * ny, nz),) * 2 + (shape(n * nx + 8, nz),) * 2
    owned = lambda dtype: pltpu.VMEM((blocks, LANES), dtype)

    hits, coef, slots = call(
        owner_first,
        (shape(512, 128), shape(5, blocks, LANES), shape(2, blocks, LANES, dtype=I32)),
        8,
        scratch=[
            owned(F32), owned(F32), owned(F32), owned(I32),
            pltpu.VMEM((2 * blocks, 128), I32), owned(I32), owned(F32),
            pltpu.SemaphoreType.DMA((7,)),
            pltpu.VMEM((10, blocks, LANES), F32),
        ],
        smem=(0,),
        remote=range(1, 8),
        microseconds=6,
        vmem=64 * 1024 * 1024 - 4096,
    )(
        block_counts, frac_start, frac_store, frac_cond, segment_ids,
        hit_tile.reshape(2 * blocks, 128), hit_cell, hit_weight,
    )
    hits = deliver(hits)
    around = swap(call(rock_faces, faces_of(2), 2)(perm, start))
    sums, cells = call(
        tile_scatter,
        (shape(4, rows, nz), shape(2, PAD_RANKS, LANES, dtype=I32)),
        1,
        scratch=[pltpu.VMEM((8, PAD_RANKS, LANES), F32)],
        microseconds=4,
    )(hits)
    found = pltpu.VMEM((2 * PAD_RANKS, LANES), F32)
    y_side, x_side = shape(4 * nx, nz), shape(4 * ny, nz)
    seen, first, sums, faces, known, x_a, x_b = call(
        tile_first,
        (shape(256, 128), field, shape(3, rows, nz), shape(6, rows, nz), field, x_side, x_side),
        9,
        scratch=[found],
        microseconds=4,
    )(sums, cells, perm, start, storage, *around)
    seen = deliver(seen)
    beside_x = trade(x_b, "flow", False), trade(x_a, "flow", True)

    pushed, partial = call(
        owner_middle,
        (shape(256, 128), shape(blocks, LANES)),
        6,
        remote=(4, 5),
        scratch=[
            pltpu.VMEM((blocks, LANES, LANES), BF16),
            pltpu.VMEM((2, blocks, LANES), F32),
            pltpu.VMEM((4, blocks, LANES), F32),
        ],
        microseconds=5,
    )(seen, frac_start, coef, slots, *beside_x)
    pushed = deliver(pushed)
    second, y_a, y_b = call(tile_second, (field, y_side, y_side), 7, remote=(6,))(
        known, first, sums, faces, *beside_x, partial
    )
    beside_y = trade(y_b, "cross", False), trade(y_a, "cross", True)

    hits = call(
        tile_scatter_again,
        shape(2, rows, nz),
        2,
        scratch=[pltpu.VMEM((4, PAD_RANKS, LANES), F32)],
        microseconds=3,
    )(pushed, cells)
    seen, third, last, *sides = call(
        tile_third,
        (shape(256, 128), field, field) + faces_of(1),
        10,
        scratch=[found],
        microseconds=4,
    )(hits, second, first, sums, faces, cells, *beside_y, *beside_x)
    seen = deliver(seen)
    around = swap(sides)
    frac, fourth = call(
        last_pair,
        (shape(blocks, LANES), field),
        12,
        scratch=[pltpu.VMEM((2, blocks, LANES), F32)],
        microseconds=4,
    )(seen, coef, slots, partial, third, last, sums, faces, *around)
    return fourth.reshape(nx, ny, nz), frac


def solution(mesh):
    grid = P("flow", "cross", None)
    owner = P(("flow", "cross"), None)
    counts, tiles = P(("flow", "cross")), P(("flow", "cross"), None, None)
    in_specs = (grid,) * 3 + (owner,) * 4 + (counts, tiles, owner, owner)
    return jax.shard_map(
        on_device, mesh=mesh, in_specs=in_specs, out_specs=(grid, owner), check_vma=False
    )
```

```python
import jax
import jax.numpy as jnp
from jax import lax
from jax.experimental import pallas as pl
from jax.experimental.pallas import tpu as pltpu
from jax.sharding import PartitionSpec as P

F32 = jnp.float32
BF16 = jnp.bfloat16
I32 = jnp.int32
I16 = jnp.int16

LANES = 256
HALF_RANKS = 36
PAD_RANKS = 40
ROWS = 64
VMEM_LIMIT = 40 * 1024 * 1024

NN = (((1,), (0,)), ((), ()))
NT = (((1,), (1,)), ((), ()))


def call(body, out_shape, n_in, scratch=(), smem=(), remote=(), microseconds=1, vmem=VMEM_LIMIT):
    def place(i):
        if i in smem:
            return pltpu.SMEM
        return pltpu.HBM if i in remote else pltpu.VMEM

    out_specs = jax.tree.map(lambda _: pl.BlockSpec(memory_space=pltpu.VMEM), out_shape)
    return pl.pallas_call(
        body,
        out_shape=out_shape,
        in_specs=[pl.BlockSpec(memory_space=place(i)) for i in range(n_in)],
        out_specs=out_specs,
        scratch_shapes=list(scratch),
        compiler_params=pltpu.CompilerParams(vmem_limit_bytes=vmem),
        cost_estimate=pl.CostEstimate(
            flops=0, bytes_accessed=int(microseconds * 3_000_000), transcendentals=0
        ),
    )


def shape(*dims, dtype=F32):
    return jax.ShapeDtypeStruct(dims, dtype)


def halves(value):
    high = value.astype(BF16).astype(F32)
    return high, value - high


def hot_rows(index_row, count):
    place = lax.broadcasted_iota(I16, (16, LANES), 0)
    index = jnp.broadcast_to(index_row, (16, LANES)).astype(I16)
    one, none = jnp.ones((16, LANES), BF16), jnp.zeros((16, LANES), BF16)
    return jnp.concatenate(
        [jnp.where(place == index - jnp.int16(16 * j), one, none) for j in range(count // 16)], axis=0
    )


def same(index_row, count):
    return lax.broadcasted_iota(I32, (count, LANES), 0) == index_row


def shift_right(x):
    return pltpu.roll(x, 1, 1)


def shift_left(x):
    return pltpu.roll(x, LANES - 1, 1)


def store_slots(out_ref, by_slot, group, groups):
    rows = by_slot.shape[0]
    if rows < 128:
        by_slot = jnp.concatenate([by_slot, jnp.zeros((128 - rows, LANES), F32)], axis=0)
    turned = by_slot.T
    for part in range(2):
        out_ref[pl.ds(group * 2 + part, 128, stride=2 * groups), :] = turned[
            part * 128 : part * 128 + 128
        ]


def load_slots(in_ref, group, groups):
    parts = [in_ref[pl.ds(group * 2 + part, 128, stride=2 * groups), :] for part in range(2)]
    return jnp.concatenate(parts, axis=0).T


def spread_ranks(split, b, rank_half):
    mine = same(rank_half, PAD_RANKS)
    rows = [jnp.where(mine, split[v, b : b + 1, :], 0.0) for v in range(split.shape[0])]
    return jnp.concatenate(rows, axis=0).astype(BF16)


def joined(total, height, count):
    return [
        total[2 * v * height : (2 * v + 1) * height] + total[(2 * v + 1) * height : (2 * v + 2) * height]
        for v in range(count)
    ]


def put_split(split, v, value):
    high, low = halves(value)
    split[2 * v] = high
    split[2 * v + 1] = low


def owner_first(
    count_ref, start_hbm, store_hbm, cond_hbm, seg_hbm, tile_hbm, cell_hbm, weight_hbm,
    out_ref, coef_ref, slot_ref,
    start_ref, store_ref, cond_ref, seg_ref, tile_ref, cell_ref, weight_ref, arrived, split,
):
    pairs = [
        (tile_hbm, tile_ref), (seg_hbm, seg_ref), (cond_hbm, cond_ref), (weight_hbm, weight_ref),
        (store_hbm, store_ref), (start_hbm, start_ref), (cell_hbm, cell_ref),
    ]
    copies = [pltpu.make_async_copy(a, b, arrived.at[i]) for i, (a, b) in enumerate(pairs)]
    for copy in copies:
        copy.start()
    for copy in copies:
        copy.wait()
    blocks = start_ref.shape[0]
    size = (blocks, LANES)
    live = lax.broadcasted_iota(I32, size, 0) < count_ref[0]
    lane = lax.broadcasted_iota(I32, size, 1)
    start = start_ref[...]
    store = store_ref[...]
    weight = jnp.where(live, weight_ref[...], 0.0)
    seg = seg_ref[...]
    linked = (seg == shift_left(seg)) & (lane < LANES - 1)
    right = jnp.where(linked, cond_ref[...], 0.0)
    left = shift_right(right)
    inverse = 1.0 / (store + left + right + weight)
    own = jnp.where(live, store * start * inverse, start)
    left = jnp.where(live, left * inverse, 0.0)
    right = jnp.where(live, right * inverse, 0.0)
    pull = weight * inverse
    coef_ref[0] = own
    coef_ref[1] = left
    coef_ref[2] = right
    coef_ref[3] = pull
    coef_ref[4] = weight
    partial = own + left * shift_right(start) + right * shift_left(start)
    put_split(split, 0, cell_ref[...].astype(F32))
    put_split(split, 1, weight)
    put_split(split, 2, weight * start)
    put_split(split, 3, weight * partial)
    put_split(split, 4, weight * pull)
    tile = jnp.concatenate(
        [tile_ref[pl.ds(0, blocks, stride=2), :], tile_ref[pl.ds(1, blocks, stride=2), :]], axis=1
    )
    slot_ref[0] = jnp.where(live, tile, -1)
    upper = jnp.where(
        lax.broadcasted_iota(I32, (LANES, LANES), 0) <= lax.broadcasted_iota(I32, (LANES, LANES), 1),
        1.0, 0.0,
    ).astype(BF16)
    before = jnp.zeros((128, LANES), F32)
    for b in range(blocks):
        target = slot_ref[0, b : b + 1, :]
        mine = same(target, 128)
        running = lax.dot_general(
            jnp.where(mine, 1.0, 0.0).astype(BF16), upper, NN, preferred_element_type=F32
        )
        rank = jnp.sum(jnp.where(mine, running + before, 0.0), axis=0, keepdims=True).astype(I32) - 1
        before += jnp.broadcast_to(running[:, LANES - 1 :], (128, LANES))
        slot_ref[1, b : b + 1, :] = jnp.maximum(rank, 0)
    target, rank = slot_ref[0], slot_ref[1]
    slot_ref[0] = jnp.where(live, target + (rank & 1) * 128, -1)
    slot_ref[1] = rank >> 1
    total = jnp.zeros((10 * PAD_RANKS, LANES), F32)
    for b in range(blocks):
        total += lax.dot_general(
            spread_ranks(split, b, slot_ref[1, b : b + 1, :]),
            hot_rows(slot_ref[0, b : b + 1, :], LANES), NT, preferred_element_type=F32,
        )
    sums = joined(total, PAD_RANKS, 5)
    store_slots(out_ref, jnp.concatenate(sums[:3], axis=0), 0, 2)
    store_slots(out_ref, jnp.concatenate(sums[3:], axis=0), 1, 2)


def unpack(recv_ref, slot_ref, key_hot, seen, blocks):
    turned = load_slots(recv_ref, 0, 1)[: 2 * PAD_RANKS]
    table = jnp.concatenate(halves(turned), axis=0).astype(BF16)
    for b in range(blocks):
        hot = hot_rows(slot_ref[0, b : b + 1, :], LANES)
        if key_hot is not None:
            key_hot[b] = hot
        found = lax.dot_general(table, hot, NN, preferred_element_type=F32)
        found = found[: 2 * PAD_RANKS] + found[2 * PAD_RANKS :]
        mine = same(slot_ref[1, b : b + 1, :], PAD_RANKS)
        for v in range(2):
            part = jnp.where(mine, found[v * PAD_RANKS : (v + 1) * PAD_RANKS], 0.0)
            seen[v, b : b + 1, :] = jnp.sum(part, axis=0, keepdims=True)


def owner_middle(
    recv_ref, start_ref, coef_ref, slot_ref, x_b, x_a, out_ref, partial_ref, key_hot, seen, split
):
    blocks = start_ref.shape[0]
    unpack(recv_ref, slot_ref, key_hot, seen, blocks)
    own, left, right, pull, weight = [coef_ref[i] for i in range(5)]
    now = start_ref[...]
    for v in range(2):
        now = own + left * shift_right(now) + right * shift_left(now) + pull * seen[v]
    partial = own + left * shift_right(now) + right * shift_left(now)
    partial_ref[...] = partial
    put_split(split, 0, weight * now)
    put_split(split, 1, weight * partial)
    total = jnp.zeros((4 * PAD_RANKS, LANES), F32)
    for b in range(blocks):
        total += lax.dot_general(
            spread_ranks(split, b, slot_ref[1, b : b + 1, :]), key_hot[b], NT,
            preferred_element_type=F32,
        )
    store_slots(out_ref, jnp.concatenate(joined(total, PAD_RANKS, 2), axis=0), 0, 1)


def fold(field):
    return jnp.concatenate([field[:, :LANES], field[:, LANES:]], axis=0)


def unfold(rows):
    half = ROWS // 2
    return jnp.concatenate([rows[:half], rows[half:]], axis=1)


def gather_cells(fields, cell_ref, found_ref):
    parts = []
    for field in fields:
        parts += halves(fold(field))
    table = jnp.concatenate(parts, axis=0).astype(BF16)
    for r in range(HALF_RANKS):
        mine = same(cell_ref[0, r : r + 1, :], ROWS)
        hot = hot_rows(cell_ref[1, r : r + 1, :], LANES)
        found = lax.dot_general(table, hot, NN, preferred_element_type=F32)
        for v, both in enumerate(joined(found, ROWS, len(fields))):
            found_ref[v * PAD_RANKS + r : v * PAD_RANKS + r + 1, :] = jnp.sum(
                jnp.where(mine, both, 0.0), axis=0, keepdims=True
            )


def scatter_cells(split, count, cell_ref, sums_ref):
    place = lax.broadcasted_iota(I16, (16, LANES), 0)
    none = jnp.zeros((16, LANES), BF16)
    total = jnp.zeros((2 * count * ROWS, LANES), F32)
    for r in range(HALF_RANKS):
        row = jnp.broadcast_to(cell_ref[0, r : r + 1, :], (16, LANES)).astype(I16)
        mine = [place == row - jnp.int16(16 * j) for j in range(ROWS // 16)]
        rows = []
        for v in range(2 * count):
            value = jnp.broadcast_to(split[v, r : r + 1, :], (16, LANES)).astype(BF16)
            rows += [jnp.where(m, value, none) for m in mine]
        hot = hot_rows(cell_ref[1, r : r + 1, :], LANES)
        total += lax.dot_general(
            jnp.concatenate(rows, axis=0), hot, NT, preferred_element_type=F32
        )
    for v, both in enumerate(joined(total, ROWS, count)):
        sums_ref[v] = unfold(both)


def pick(odd, yes, no):
    return jnp.where(odd, yes, no)


def parity():
    return lax.axis_index("flow") % 2 == 1, lax.axis_index("cross") % 2 == 1


def y_layer(field, y):
    return jnp.concatenate([field[i + y : i + y + 1] for i in range(0, field.shape[0], 8)], axis=0)


def widen(layer):
    rows, nz = layer.shape
    return jnp.concatenate(
        [jnp.broadcast_to(layer[i : i + 1], (8, nz)) for i in range(rows)], axis=0
    )


def put_faces(field, refs, place=0):
    rows = field.shape[0]
    odd_x, odd_y = parity()
    x_low, x_high = field[:8], field[rows - 8 :]
    y_low, y_high = y_layer(field, 0), y_layer(field, 7)
    at_x, at_y = pl.ds(place * 8, 8), pl.ds(place * (rows // 8), rows // 8)
    refs[0][at_x, :] = pick(odd_x, x_low, x_high)
    refs[1][at_x, :] = pick(odd_x, x_high, x_low)
    refs[2][at_y, :] = pick(odd_y, y_low, y_high)
    refs[3][at_y, :] = pick(odd_y, y_high, y_low)
    for ref in refs[2:]:
        ref[ref.shape[0] - 8 :, :] = jnp.zeros((8, field.shape[1]), F32)


def sides_of(refs, place=0, rows=32):
    odd_x, odd_y = parity()
    at_x, at_y = pl.ds(place * 8, 8), pl.ds(place * (rows // 8), rows // 8)
    x_first, x_second = refs[0][at_x, :], refs[1][at_x, :]
    y_first, y_second = refs[2][at_y, :], refs[3][at_y, :]
    return (
        pick(odd_x, x_first, x_second),
        pick(odd_x, x_second, x_first),
        pick(odd_y, y_first, y_second),
        pick(odd_y, y_second, y_first),
    )


def rock_faces(perm_ref, start_ref, *sides):
    put_faces(perm_ref[...], sides, 0)
    put_faces(start_ref[...], sides, 1)


def neighbours(field, x_low, x_high, y_low, y_high, ny):
    rows, nz = field.shape
    nx = rows // ny
    west = jnp.concatenate([x_low, field[: rows - ny]], axis=0)
    east = jnp.concatenate([field[ny:], x_high], axis=0)
    place = lax.broadcasted_iota(I32, (rows, nz), 0) % ny
    wide_low = jnp.concatenate(
        [jnp.broadcast_to(y_low[i : i + 1], (ny, nz)) for i in range(nx)], axis=0
    )
    wide_high = jnp.concatenate(
        [jnp.broadcast_to(y_high[i : i + 1], (ny, nz)) for i in range(nx)], axis=0
    )
    south = jnp.where(place == 0, wide_low, pltpu.roll(field, 1, 0))
    north = jnp.where(place == ny - 1, wide_high, pltpu.roll(field, rows - 1, 0))
    below = pltpu.roll(field, 1, 1)
    above = pltpu.roll(field, nz - 1, 1)
    return west, east, south, north, below, above


def tile_scatter(recv_ref, sums_ref, cells_ref, split):
    first = load_slots(recv_ref, 0, 2)
    second = load_slots(recv_ref, 1, 2)
    cell = first[:PAD_RANKS].astype(I32)
    deep = cell & 511
    cells_ref[0] = ((deep >> 8) << 5) + (cell >> 9)
    cells_ref[1] = deep & (LANES - 1)
    put_split(split, 0, first[PAD_RANKS : 2 * PAD_RANKS])
    put_split(split, 1, first[2 * PAD_RANKS : 3 * PAD_RANKS])
    put_split(split, 2, second[:PAD_RANKS])
    put_split(split, 3, second[PAD_RANKS : 2 * PAD_RANKS])
    scatter_cells(split, 4, cells_ref, sums_ref)


def tile_first(hits_ref, cells_ref, perm_ref, start_ref, storage_ref, yh, xh, yl, xl,
               out_ref, next_ref, sums_ref, faces_ref, known_ref, x_a, x_b, found):
    rows, nz = perm_ref.shape
    ny = 8
    perm = perm_ref[...]
    start = start_ref[...]
    beside = neighbours(perm, *sides_of((xl, xh, yl, yh), 0), ny)
    around = neighbours(start, *sides_of((xl, xh, yl, yh), 1), ny)
    i_flow, i_cross = lax.axis_index("flow"), lax.axis_index("cross")
    row = lax.broadcasted_iota(I32, (rows, nz), 0)
    lane = lax.broadcasted_iota(I32, (rows, nz), 1)
    closed = [
        (row < ny) & (i_flow == 0),
        (row >= rows - ny) & (i_flow == lax.axis_size("flow") - 1),
        (row % ny == 0) & (i_cross == 0),
        (row % ny == ny - 1) & (i_cross == lax.axis_size("cross") - 1),
        lane == 0,
        lane == nz - 1,
    ]
    storage = storage_ref[...]
    base = storage * start
    inflow = jnp.zeros_like(start)
    total = storage + hits_ref[0]
    for i in range(6):
        face = jnp.where(closed[i], 0.0, 2.0 * perm * beside[i] / (perm + beside[i]))
        faces_ref[i] = face
        total += face
        inflow += face * around[i]
    inverse = 1.0 / total
    now = (base + inflow + hits_ref[1]) * inverse
    next_ref[...] = now
    sums_ref[0] = inverse
    sums_ref[1] = base
    sums_ref[2] = hits_ref[3]
    far, near = jnp.zeros((ny, nz), F32), jnp.zeros((rows // ny, nz), F32)
    within = neighbours(now, far, far, near, near, ny)
    inflow = base + hits_ref[2] + start * hits_ref[3]
    for i in range(6):
        inflow += faces_ref[i] * within[i]
    known = inflow * inverse
    known_ref[...] = known
    south, north = faces_ref[2] * inverse, faces_ref[3] * inverse
    spare = jnp.zeros((6, nz), F32)
    odd_x, _ = parity()
    sides = []
    for x, face in ((0, 0), (rows // ny - 1, 1)):
        at, end = x * ny, x * ny + ny
        layers = [a[at:end] for a in (now, known, faces_ref[face] * inverse)]
        sides.append(
            jnp.concatenate(layers + [south[at : at + 1], north[end - 1 : end], spare], axis=0)
        )
    x_a[...] = pick(odd_x, sides[0], sides[1])
    x_b[...] = pick(odd_x, sides[1], sides[0])
    found[...] = jnp.zeros_like(found)
    gather_cells([start, now], cells_ref, found)
    store_slots(out_ref, found[...], 0, 1)


def flow_in(field, faces_ref, xl, xh, yl, yh):
    around = neighbours(field, *sides_of((xl, xh, yl, yh)), 8)
    total = faces_ref[0] * around[0]
    for i in range(1, 6):
        total += faces_ref[i] * around[i]
    return total


def tile_second(known_ref, now_ref, sums_ref, faces_ref, x_b, x_a, after, next_ref, y_a, y_b):
    odd_x, odd_y = parity()
    x_low, x_high = pick(odd_x, x_a[...], x_b[...]), pick(odd_x, x_b[...], x_a[...])
    now, inverse = now_ref[...], sums_ref[0]
    rows, nz = now.shape
    idle = jnp.zeros((rows - 16, nz), F32)
    west, east = faces_ref[0] * inverse, faces_ref[1] * inverse
    later = known_ref[...] + jnp.concatenate(
        [west[:8] * x_low[:8], idle, east[rows - 8 :] * x_high[:8]], axis=0
    )
    next_ref[...] = later
    spare = jnp.zeros((2, nz), F32)
    sides = []
    for y, face in ((0, 2), (7, 3)):
        layers = [y_layer(a, y) for a in (now, later, faces_ref[face] * inverse)]
        corners = [x_low[y : y + 1], x_high[y : y + 1]]
        sides.append(jnp.concatenate(layers + corners + [spare], axis=0))
    y_a[...] = pick(odd_y, sides[0], sides[1])
    y_b[...] = pick(odd_y, sides[1], sides[0])


def tile_scatter_again(recv_ref, cells_ref, sums_ref, split):
    turned = load_slots(recv_ref, 0, 1)
    put_split(split, 0, turned[:PAD_RANKS])
    put_split(split, 1, turned[PAD_RANKS : 2 * PAD_RANKS])
    scatter_cells(split, 2, cells_ref, sums_ref)


def tile_third(hits_ref, part_ref, before_ref, sums_ref, faces_ref, cells_ref, y_b, y_a, x_b, x_a,
               out_ref, next_ref, last_ref, a, b, c, d, found):
    odd_x, odd_y = parity()
    x_low, x_high = pick(odd_x, x_a[...], x_b[...]), pick(odd_x, x_b[...], x_a[...])
    y_low, y_high = pick(odd_y, y_a[...], y_b[...]), pick(odd_y, y_b[...], y_a[...])
    before, inverse = before_ref[...], sums_ref[0]
    rows, nz = before.shape
    nx = rows // 8
    y = lax.broadcasted_iota(I32, (rows, nz), 0) % 8
    inflow = jnp.where(y == 0, faces_ref[2] * widen(y_low[:nx]), 0.0)
    inflow += jnp.where(y == 7, faces_ref[3] * widen(y_high[:nx]), 0.0)
    now = part_ref[...] + inflow * inverse
    sides = []
    still = jnp.zeros((6, nz), F32)
    for i, (side, at) in enumerate(((x_low, 0), (x_high, rows - 8))):
        corner = slice(3 * nx + i, 3 * nx + i + 1)
        corners = [side[24:25] * y_low[corner], still, side[25:26] * y_high[corner]]
        sides.append(
            side[8:16] + side[16:24] * before[at : at + 8] + jnp.concatenate(corners, axis=0)
        )
    for side, at in ((y_low, 0), (y_high, 7)):
        sides.append(side[nx : 2 * nx] + side[2 * nx : 3 * nx] * y_layer(before, at))
    around = neighbours(now, *sides, 8)
    inflow = sums_ref[1] + hits_ref[0]
    for i in range(6):
        inflow += faces_ref[i] * around[i]
    later = inflow * inverse
    next_ref[...] = later
    put_faces(later, (a, b, c, d))
    last_ref[...] = sums_ref[1] + hits_ref[1] + now * sums_ref[2]
    found[...] = jnp.zeros_like(found)
    gather_cells([now, later], cells_ref, found)
    store_slots(out_ref, found[...], 0, 1)


def last_pair(recv_ref, coef_ref, slot_ref, partial_ref, now_ref, last_ref, sums_ref, faces_ref,
              yh, xh, yl, xl, frac_ref, matrix_ref, seen):
    inflow = flow_in(now_ref[...], faces_ref, xl, xh, yl, yh)
    matrix_ref[...] = (last_ref[...] + inflow) * sums_ref[0]
    blocks = partial_ref.shape[0]
    unpack(recv_ref, slot_ref, None, seen, blocks)
    own, left, right, pull = [coef_ref[i] for i in range(4)]
    now = partial_ref[...] + pull * seen[0]
    frac_ref[...] = own + left * shift_right(now) + right * shift_left(now) + pull * seen[1]


def trade(block, axis, first):
    flow, cross = lax.axis_size("flow"), lax.axis_size("cross")
    if flow * cross == 1:
        return block
    step, count = (cross, flow) if axis == "flow" else (1, cross)
    pairs = []
    for i in range(flow * cross):
        at = i // step % count
        to = at + 1 if (at % 2 == 0) == first else at - 1
        other = i ^ (1 if axis == "flow" else cross)
        pairs.append((i, i + (to - at) * step if 0 <= to < count else other))
    return lax.ppermute(block, ("flow", "cross"), pairs)


def swap(faces):
    y_first = trade(faces[2], "cross", True)
    y_second = trade(faces[3], "cross", False)
    x_first = trade(faces[0], "flow", True)
    x_second = trade(faces[1], "flow", False)
    return y_second, x_second, y_first, x_first


def deliver(payload):
    return lax.all_to_all(payload, ("flow", "cross"), split_axis=0, concat_axis=0, tiled=True)


def on_device(
    matrix_start, storage, perm, frac_start, frac_store, frac_cond,
    segment_ids, block_counts, hit_tile, hit_cell, hit_weight,
):
    blocks = frac_start.shape[0]
    nx, ny, nz = matrix_start.shape
    rows = nx * ny
    start, storage, perm = [a.reshape(rows, nz) for a in (matrix_start, storage, perm)]
    field = shape(rows, nz)
    faces_of = lambda n: (shape(n * ny, nz),) * 2 + (shape(n * nx + 8, nz),) * 2
    owned = lambda dtype: pltpu.VMEM((blocks, LANES), dtype)

    hits, coef, slots = call(
        owner_first,
        (shape(512, 128), shape(5, blocks, LANES), shape(2, blocks, LANES, dtype=I32)),
        8,
        scratch=[
            owned(F32), owned(F32), owned(F32), owned(I32),
            pltpu.VMEM((2 * blocks, 128), I32), owned(I32), owned(F32),
            pltpu.SemaphoreType.DMA((7,)),
            pltpu.VMEM((10, blocks, LANES), F32),
        ],
        smem=(0,),
        remote=range(1, 8),
        microseconds=6,
        vmem=64 * 1024 * 1024 - 4096,
    )(
        block_counts, frac_start, frac_store, frac_cond, segment_ids,
        hit_tile.reshape(2 * blocks, 128), hit_cell, hit_weight,
    )
    hits = deliver(hits)
    around = swap(call(rock_faces, faces_of(2), 2)(perm, start))
    sums, cells = call(
        tile_scatter,
        (shape(4, rows, nz), shape(2, PAD_RANKS, LANES, dtype=I32)),
        1,
        scratch=[pltpu.VMEM((8, PAD_RANKS, LANES), F32)],
        microseconds=4,
    )(hits)
    found = pltpu.VMEM((2 * PAD_RANKS, LANES), F32)
    y_side, x_side = shape(4 * nx, nz), shape(4 * ny, nz)
    seen, first, sums, faces, known, x_a, x_b = call(
        tile_first,
        (shape(256, 128), field, shape(3, rows, nz), shape(6, rows, nz), field, x_side, x_side),
        9,
        scratch=[found],
        microseconds=4,
    )(sums, cells, perm, start, storage, *around)
    seen = deliver(seen)
    beside_x = trade(x_b, "flow", False), trade(x_a, "flow", True)

    pushed, partial = call(
        owner_middle,
        (shape(256, 128), shape(blocks, LANES)),
        6,
        remote=(4, 5),
        scratch=[
            pltpu.VMEM((blocks, LANES, LANES), BF16),
            pltpu.VMEM((2, blocks, LANES), F32),
            pltpu.VMEM((4, blocks, LANES), F32),
        ],
        microseconds=5,
    )(seen, frac_start, coef, slots, *beside_x)
    pushed = deliver(pushed)
    second, y_a, y_b = call(tile_second, (field, y_side, y_side), 7, remote=(6,))(
        known, first, sums, faces, *beside_x, partial
    )
    beside_y = trade(y_b, "cross", False), trade(y_a, "cross", True)

    hits = call(
        tile_scatter_again,
        shape(2, rows, nz),
        2,
        scratch=[pltpu.VMEM((4, PAD_RANKS, LANES), F32)],
        microseconds=3,
    )(pushed, cells)
    seen, third, last, *sides = call(
        tile_third,
        (shape(256, 128), field, field) + faces_of(1),
        10,
        scratch=[found],
        microseconds=4,
    )(hits, second, first, sums, faces, cells, *beside_y, *beside_x)
    seen = deliver(seen)
    around = swap(sides)
    frac, fourth = call(
        last_pair,
        (shape(blocks, LANES), field),
        12,
        scratch=[pltpu.VMEM((2, blocks, LANES), F32)],
        microseconds=4,
    )(seen, coef, slots, partial, third, last, sums, faces, *around)
    return fourth.reshape(nx, ny, nz), frac


def solution(mesh):
    grid = P("flow", "cross", None)
    owner = P(("flow", "cross"), None)
    counts, tiles = P(("flow", "cross")), P(("flow", "cross"), None, None)
    in_specs = (grid,) * 3 + (owner,) * 4 + (counts, tiles, owner, owner)
    return jax.shard_map(
        on_device, mesh=mesh, in_specs=in_specs, out_specs=(grid, owner), check_vma=False
    )
```

```python
import jax
import jax.numpy as jnp
from jax import lax
from jax.experimental import pallas as pl
from jax.experimental.pallas import tpu as pltpu
from jax.sharding import PartitionSpec as P

F32 = jnp.float32
BF16 = jnp.bfloat16
I32 = jnp.int32
I16 = jnp.int16

LANES = 256
HALF_RANKS = 36
PAD_RANKS = 40
ROWS = 64
VMEM_LIMIT = 40 * 1024 * 1024

NN = (((1,), (0,)), ((), ()))
NT = (((1,), (1,)), ((), ()))


def call(body, out_shape, n_in, scratch=(), smem=(), remote=(), microseconds=1, vmem=VMEM_LIMIT, early=False):
    def place(i):
        if i in smem:
            return pltpu.SMEM
        return pltpu.HBM if i in remote else pltpu.VMEM

    out_specs = jax.tree.map(lambda _: pl.BlockSpec(memory_space=pltpu.VMEM), out_shape)
    if early:
        out_specs = (pl.BlockSpec(memory_space=pltpu.HBM),) + tuple(out_specs[1:])
    return pl.pallas_call(
        body,
        out_shape=out_shape,
        in_specs=[pl.BlockSpec(memory_space=place(i)) for i in range(n_in)],
        out_specs=out_specs,
        scratch_shapes=list(scratch),
        compiler_params=pltpu.CompilerParams(vmem_limit_bytes=vmem),
        cost_estimate=pl.CostEstimate(
            flops=0, bytes_accessed=int(microseconds * 3_000_000), transcendentals=0
        ),
    )


def shape(*dims, dtype=F32):
    return jax.ShapeDtypeStruct(dims, dtype)


def halves(value):
    high = value.astype(BF16).astype(F32)
    return high, value - high


def hot_rows(index_row, count):
    place = lax.broadcasted_iota(I16, (16, LANES), 0)
    index = jnp.broadcast_to(index_row, (16, LANES)).astype(I16)
    one, none = jnp.ones((16, LANES), BF16), jnp.zeros((16, LANES), BF16)
    return jnp.concatenate(
        [jnp.where(place == index - jnp.int16(16 * j), one, none) for j in range(count // 16)], axis=0
    )


def same(index_row, count):
    return lax.broadcasted_iota(I32, (count, LANES), 0) == index_row


def shift_right(x):
    return pltpu.roll(x, 1, 1)


def shift_left(x):
    return pltpu.roll(x, LANES - 1, 1)


def store_slots(out_ref, by_slot, group, groups):
    rows = by_slot.shape[0]
    if rows < 128:
        by_slot = jnp.concatenate([by_slot, jnp.zeros((128 - rows, LANES), F32)], axis=0)
    turned = by_slot.T
    for part in range(2):
        out_ref[pl.ds(group * 2 + part, 128, stride=2 * groups), :] = turned[
            part * 128 : part * 128 + 128
        ]


def load_slots(in_ref, group, groups):
    parts = [in_ref[pl.ds(group * 2 + part, 128, stride=2 * groups), :] for part in range(2)]
    return jnp.concatenate(parts, axis=0).T


def spread_ranks(split, b, rank_half):
    mine = same(rank_half, PAD_RANKS)
    rows = [jnp.where(mine, split[v, b : b + 1, :], 0.0) for v in range(split.shape[0])]
    return jnp.concatenate(rows, axis=0).astype(BF16)


def joined(total, height, count):
    return [
        total[2 * v * height : (2 * v + 1) * height] + total[(2 * v + 1) * height : (2 * v + 2) * height]
        for v in range(count)
    ]


def put_split(split, v, value):
    high, low = halves(value)
    split[2 * v] = high
    split[2 * v + 1] = low


def owner_first(
    count_ref, start_hbm, store_hbm, cond_hbm, seg_hbm, tile_hbm, cell_hbm, weight_hbm,
    out_ref, coef_ref, slot_ref,
    start_ref, store_ref, cond_ref, seg_ref, tile_ref, cell_ref, weight_ref, arrived, split,
):
    pairs = [
        (tile_hbm, tile_ref), (seg_hbm, seg_ref), (cond_hbm, cond_ref), (weight_hbm, weight_ref),
        (store_hbm, store_ref), (start_hbm, start_ref), (cell_hbm, cell_ref),
    ]
    copies = [pltpu.make_async_copy(a, b, arrived.at[i]) for i, (a, b) in enumerate(pairs)]
    for copy in copies:
        copy.start()
    blocks = start_ref.shape[0]
    size = (blocks, LANES)
    live = lax.broadcasted_iota(I32, size, 0) < count_ref[0]
    lane = lax.broadcasted_iota(I32, size, 1)
    copies[0].wait()
    tile = jnp.concatenate(
        [tile_ref[pl.ds(0, blocks, stride=2), :], tile_ref[pl.ds(1, blocks, stride=2), :]], axis=1
    )
    target = jnp.where(live, tile, -1)
    slot_ref[0] = target
    upper = jnp.where(
        lax.broadcasted_iota(I32, (LANES, LANES), 0) <= lax.broadcasted_iota(I32, (LANES, LANES), 1),
        1.0, 0.0,
    ).astype(BF16)
    before = jnp.zeros((128, LANES), F32)
    for b in range(blocks):
        mine = hot_rows(slot_ref[0, b : b + 1, :], 128)
        running = lax.dot_general(mine, upper, NN, preferred_element_type=F32)
        rank = jnp.sum(mine.astype(F32) * (running + before), axis=0, keepdims=True)
        before += jnp.broadcast_to(running[:, LANES - 1 :], (128, LANES))
        slot_ref[1, b : b + 1, :] = rank.astype(I32)
    rank = jnp.maximum(slot_ref[1] - 1, 0)
    slot_ref[0] = jnp.where(live, target + (rank & 1) * 128, -1)
    slot_ref[1] = rank >> 1
    for copy in copies[1:]:
        copy.wait()
    start = start_ref[...]
    store = store_ref[...]
    weight = jnp.where(live, weight_ref[...], 0.0)
    seg = seg_ref[...]
    linked = (seg == shift_left(seg)) & (lane < LANES - 1)
    right = jnp.where(linked, cond_ref[...], 0.0)
    left = shift_right(right)
    inverse = 1.0 / (store + left + right + weight)
    own = jnp.where(live, store * start * inverse, start)
    left = jnp.where(live, left * inverse, 0.0)
    right = jnp.where(live, right * inverse, 0.0)
    pull = weight * inverse
    coef_ref[0] = own
    coef_ref[1] = left
    coef_ref[2] = right
    coef_ref[3] = pull
    coef_ref[4] = weight
    partial = own + left * shift_right(start) + right * shift_left(start)
    put_split(split, 0, cell_ref[...].astype(F32))
    put_split(split, 1, weight)
    put_split(split, 2, weight * start)
    put_split(split, 3, weight * partial)
    put_split(split, 4, weight * pull)
    total = jnp.zeros((10 * PAD_RANKS, LANES), F32)
    for b in range(blocks):
        total += lax.dot_general(
            spread_ranks(split, b, slot_ref[1, b : b + 1, :]),
            hot_rows(slot_ref[0, b : b + 1, :], LANES), NT, preferred_element_type=F32,
        )
    sums = joined(total, PAD_RANKS, 5)
    store_slots(out_ref, jnp.concatenate(sums[:3], axis=0), 0, 2)
    store_slots(out_ref, jnp.concatenate(sums[3:], axis=0), 1, 2)


def unpack(recv_ref, slot_ref, key_hot, seen, blocks):
    turned = load_slots(recv_ref, 0, 1)[: 2 * PAD_RANKS]
    table = jnp.concatenate(halves(turned), axis=0).astype(BF16)
    for b in range(blocks):
        hot = hot_rows(slot_ref[0, b : b + 1, :], LANES)
        if key_hot is not None:
            key_hot[b] = hot
        found = lax.dot_general(table, hot, NN, preferred_element_type=F32)
        found = found[: 2 * PAD_RANKS] + found[2 * PAD_RANKS :]
        mine = same(slot_ref[1, b : b + 1, :], PAD_RANKS)
        for v in range(2):
            part = jnp.where(mine, found[v * PAD_RANKS : (v + 1) * PAD_RANKS], 0.0)
            seen[v, b : b + 1, :] = jnp.sum(part, axis=0, keepdims=True)


def owner_middle(
    recv_ref, start_ref, coef_ref, slot_ref, x_b, x_a, out_ref, partial_ref, key_hot, seen, split
):
    blocks = start_ref.shape[0]
    unpack(recv_ref, slot_ref, key_hot, seen, blocks)
    own, left, right, pull, weight = [coef_ref[i] for i in range(5)]
    now = start_ref[...]
    for v in range(2):
        now = own + left * shift_right(now) + right * shift_left(now) + pull * seen[v]
    partial = own + left * shift_right(now) + right * shift_left(now)
    partial_ref[...] = partial
    put_split(split, 0, weight * now)
    put_split(split, 1, weight * partial)
    total = jnp.zeros((4 * PAD_RANKS, LANES), F32)
    for b in range(blocks):
        total += lax.dot_general(
            spread_ranks(split, b, slot_ref[1, b : b + 1, :]), key_hot[b], NT,
            preferred_element_type=F32,
        )
    store_slots(out_ref, jnp.concatenate(joined(total, PAD_RANKS, 2), axis=0), 0, 1)


def fold(field):
    return jnp.concatenate([field[:, :LANES], field[:, LANES:]], axis=0)


def unfold(rows):
    half = ROWS // 2
    return jnp.concatenate([rows[:half], rows[half:]], axis=1)


def gather_cells(fields, cell_ref, found_ref):
    parts = []
    for field in fields:
        parts += halves(fold(field))
    table = jnp.concatenate(parts, axis=0).astype(BF16)
    for r in range(HALF_RANKS):
        mine = same(cell_ref[0, r : r + 1, :], ROWS)
        hot = hot_rows(cell_ref[1, r : r + 1, :], LANES)
        found = lax.dot_general(table, hot, NN, preferred_element_type=F32)
        for v, both in enumerate(joined(found, ROWS, len(fields))):
            found_ref[v * PAD_RANKS + r : v * PAD_RANKS + r + 1, :] = jnp.sum(
                jnp.where(mine, both, 0.0), axis=0, keepdims=True
            )


def scatter_cells(split, count, cell_ref, sums_ref):
    place = lax.broadcasted_iota(I16, (16, LANES), 0)
    none = jnp.zeros((16, LANES), BF16)
    total = jnp.zeros((2 * count * ROWS, LANES), F32)
    for r in range(HALF_RANKS):
        row = jnp.broadcast_to(cell_ref[0, r : r + 1, :], (16, LANES)).astype(I16)
        mine = [place == row - jnp.int16(16 * j) for j in range(ROWS // 16)]
        rows = []
        for v in range(2 * count):
            value = jnp.broadcast_to(split[v, r : r + 1, :], (16, LANES)).astype(BF16)
            rows += [jnp.where(m, value, none) for m in mine]
        hot = hot_rows(cell_ref[1, r : r + 1, :], LANES)
        total += lax.dot_general(
            jnp.concatenate(rows, axis=0), hot, NT, preferred_element_type=F32
        )
    for v, both in enumerate(joined(total, ROWS, count)):
        sums_ref[v] = unfold(both)


def pick(odd, yes, no):
    return jnp.where(odd, yes, no)


def parity():
    return lax.axis_index("flow") % 2 == 1, lax.axis_index("cross") % 2 == 1


def y_layer(field, y):
    return jnp.concatenate([field[i + y : i + y + 1] for i in range(0, field.shape[0], 8)], axis=0)


def widen(layer):
    rows, nz = layer.shape
    return jnp.concatenate(
        [jnp.broadcast_to(layer[i : i + 1], (8, nz)) for i in range(rows)], axis=0
    )


def put_faces(field, refs, place=0):
    rows = field.shape[0]
    odd_x, odd_y = parity()
    x_low, x_high = field[:8], field[rows - 8 :]
    y_low, y_high = y_layer(field, 0), y_layer(field, 7)
    at_x, at_y = pl.ds(place * 8, 8), pl.ds(place * (rows // 8), rows // 8)
    refs[0][at_x, :] = pick(odd_x, x_low, x_high)
    refs[1][at_x, :] = pick(odd_x, x_high, x_low)
    refs[2][at_y, :] = pick(odd_y, y_low, y_high)
    refs[3][at_y, :] = pick(odd_y, y_high, y_low)
    for ref in refs[2:]:
        ref[ref.shape[0] - 8 :, :] = jnp.zeros((8, field.shape[1]), F32)


def sides_of(refs, place=0, rows=32):
    odd_x, odd_y = parity()
    at_x, at_y = pl.ds(place * 8, 8), pl.ds(place * (rows // 8), rows // 8)
    x_first, x_second = refs[0][at_x, :], refs[1][at_x, :]
    y_first, y_second = refs[2][at_y, :], refs[3][at_y, :]
    return (
        pick(odd_x, x_first, x_second),
        pick(odd_x, x_second, x_first),
        pick(odd_y, y_first, y_second),
        pick(odd_y, y_second, y_first),
    )


def rock_faces(perm_ref, start_ref, *sides):
    put_faces(perm_ref[...], sides, 0)
    put_faces(start_ref[...], sides, 1)


def neighbours(field, x_low, x_high, y_low, y_high, ny):
    rows, nz = field.shape
    nx = rows // ny
    west = jnp.concatenate([x_low, field[: rows - ny]], axis=0)
    east = jnp.concatenate([field[ny:], x_high], axis=0)
    place = lax.broadcasted_iota(I32, (rows, nz), 0) % ny
    wide_low = jnp.concatenate(
        [jnp.broadcast_to(y_low[i : i + 1], (ny, nz)) for i in range(nx)], axis=0
    )
    wide_high = jnp.concatenate(
        [jnp.broadcast_to(y_high[i : i + 1], (ny, nz)) for i in range(nx)], axis=0
    )
    south = jnp.where(place == 0, wide_low, pltpu.roll(field, 1, 0))
    north = jnp.where(place == ny - 1, wide_high, pltpu.roll(field, rows - 1, 0))
    below = pltpu.roll(field, 1, 1)
    above = pltpu.roll(field, nz - 1, 1)
    return west, east, south, north, below, above


def tile_scatter(recv_ref, sums_ref, cells_ref, split):
    first = load_slots(recv_ref, 0, 2)
    second = load_slots(recv_ref, 1, 2)
    cell = first[:PAD_RANKS].astype(I32)
    deep = cell & 511
    cells_ref[0] = ((deep >> 8) << 5) + (cell >> 9)
    cells_ref[1] = deep & (LANES - 1)
    put_split(split, 0, first[PAD_RANKS : 2 * PAD_RANKS])
    put_split(split, 1, first[2 * PAD_RANKS : 3 * PAD_RANKS])
    put_split(split, 2, second[:PAD_RANKS])
    put_split(split, 3, second[PAD_RANKS : 2 * PAD_RANKS])
    scatter_cells(split, 4, cells_ref, sums_ref)


def tile_first(hits_ref, cells_ref, perm_ref, start_ref, storage_ref, yh, xh, yl, xl,
               out_ref, next_ref, sums_ref, faces_ref, known_ref, x_a, x_b, found, stage, left):
    rows, nz = perm_ref.shape
    ny = 8
    perm = perm_ref[...]
    start = start_ref[...]
    beside = neighbours(perm, *sides_of((xl, xh, yl, yh), 0), ny)
    around = neighbours(start, *sides_of((xl, xh, yl, yh), 1), ny)
    i_flow, i_cross = lax.axis_index("flow"), lax.axis_index("cross")
    row = lax.broadcasted_iota(I32, (rows, nz), 0)
    lane = lax.broadcasted_iota(I32, (rows, nz), 1)
    closed = [
        (row < ny) & (i_flow == 0),
        (row >= rows - ny) & (i_flow == lax.axis_size("flow") - 1),
        (row % ny == 0) & (i_cross == 0),
        (row % ny == ny - 1) & (i_cross == lax.axis_size("cross") - 1),
        lane == 0,
        lane == nz - 1,
    ]
    storage = storage_ref[...]
    base = storage * start
    inflow = jnp.zeros_like(start)
    total = storage + hits_ref[0]
    for i in range(6):
        face = jnp.where(closed[i], 0.0, 2.0 * perm * beside[i] / (perm + beside[i]))
        faces_ref[i] = face
        total += face
        inflow += face * around[i]
    inverse = 1.0 / total
    now = (base + inflow + hits_ref[1]) * inverse
    next_ref[...] = now
    sums_ref[0] = inverse
    sums_ref[1] = base
    sums_ref[2] = hits_ref[3]
    found[...] = jnp.zeros_like(found)
    gather_cells([start, now], cells_ref, found)
    store_slots(stage, found[...], 0, 1)
    copy = pltpu.make_async_copy(stage, out_ref, left.at[0])
    copy.start()
    far, near = jnp.zeros((ny, nz), F32), jnp.zeros((rows // ny, nz), F32)
    within = neighbours(now, far, far, near, near, ny)
    inflow = base + hits_ref[2] + start * hits_ref[3]
    for i in range(6):
        inflow += faces_ref[i] * within[i]
    known = inflow * inverse
    known_ref[...] = known
    south, north = faces_ref[2] * inverse, faces_ref[3] * inverse
    spare = jnp.zeros((6, nz), F32)
    odd_x, _ = parity()
    sides = []
    for x, face in ((0, 0), (rows // ny - 1, 1)):
        at, end = x * ny, x * ny + ny
        layers = [a[at:end] for a in (now, known, faces_ref[face] * inverse)]
        sides.append(
            jnp.concatenate(layers + [south[at : at + 1], north[end - 1 : end], spare], axis=0)
        )
    x_a[...] = pick(odd_x, sides[0], sides[1])
    x_b[...] = pick(odd_x, sides[1], sides[0])
    copy.wait()


def flow_in(field, faces_ref, xl, xh, yl, yh):
    around = neighbours(field, *sides_of((xl, xh, yl, yh)), 8)
    total = faces_ref[0] * around[0]
    for i in range(1, 6):
        total += faces_ref[i] * around[i]
    return total


def tile_second(known_ref, now_ref, sums_ref, faces_ref, x_b, x_a, after, next_ref, y_a, y_b):
    odd_x, odd_y = parity()
    x_low, x_high = pick(odd_x, x_a[...], x_b[...]), pick(odd_x, x_b[...], x_a[...])
    now, inverse = now_ref[...], sums_ref[0]
    rows, nz = now.shape
    idle = jnp.zeros((rows - 16, nz), F32)
    west, east = faces_ref[0] * inverse, faces_ref[1] * inverse
    later = known_ref[...] + jnp.concatenate(
        [west[:8] * x_low[:8], idle, east[rows - 8 :] * x_high[:8]], axis=0
    )
    next_ref[...] = later
    spare = jnp.zeros((2, nz), F32)
    sides = []
    for y, face in ((0, 2), (7, 3)):
        layers = [y_layer(a, y) for a in (now, later, faces_ref[face] * inverse)]
        corners = [x_low[y : y + 1], x_high[y : y + 1]]
        sides.append(jnp.concatenate(layers + corners + [spare], axis=0))
    y_a[...] = pick(odd_y, sides[0], sides[1])
    y_b[...] = pick(odd_y, sides[1], sides[0])


def tile_scatter_again(recv_ref, cells_ref, sums_ref, split):
    turned = load_slots(recv_ref, 0, 1)
    put_split(split, 0, turned[:PAD_RANKS])
    put_split(split, 1, turned[PAD_RANKS : 2 * PAD_RANKS])
    scatter_cells(split, 2, cells_ref, sums_ref)


def tile_third(hits_ref, part_ref, before_ref, sums_ref, faces_ref, cells_ref, y_b, y_a, x_b, x_a,
               out_ref, next_ref, last_ref, a, b, c, d, found, stage, left):
    odd_x, odd_y = parity()
    x_low, x_high = pick(odd_x, x_a[...], x_b[...]), pick(odd_x, x_b[...], x_a[...])
    y_low, y_high = pick(odd_y, y_a[...], y_b[...]), pick(odd_y, y_b[...], y_a[...])
    before, inverse = before_ref[...], sums_ref[0]
    rows, nz = before.shape
    nx = rows // 8
    y = lax.broadcasted_iota(I32, (rows, nz), 0) % 8
    inflow = jnp.where(y == 0, faces_ref[2] * widen(y_low[:nx]), 0.0)
    inflow += jnp.where(y == 7, faces_ref[3] * widen(y_high[:nx]), 0.0)
    now = part_ref[...] + inflow * inverse
    sides = []
    still = jnp.zeros((6, nz), F32)
    for i, (side, at) in enumerate(((x_low, 0), (x_high, rows - 8))):
        corner = slice(3 * nx + i, 3 * nx + i + 1)
        corners = [side[24:25] * y_low[corner], still, side[25:26] * y_high[corner]]
        sides.append(
            side[8:16] + side[16:24] * before[at : at + 8] + jnp.concatenate(corners, axis=0)
        )
    for side, at in ((y_low, 0), (y_high, 7)):
        sides.append(side[nx : 2 * nx] + side[2 * nx : 3 * nx] * y_layer(before, at))
    around = neighbours(now, *sides, 8)
    inflow = sums_ref[1] + hits_ref[0]
    for i in range(6):
        inflow += faces_ref[i] * around[i]
    later = inflow * inverse
    next_ref[...] = later
    found[...] = jnp.zeros_like(found)
    gather_cells([now, later], cells_ref, found)
    store_slots(stage, found[...], 0, 1)
    copy = pltpu.make_async_copy(stage, out_ref, left.at[0])
    copy.start()
    put_faces(later, (a, b, c, d))
    last_ref[...] = sums_ref[1] + hits_ref[1] + now * sums_ref[2]
    copy.wait()


def last_pair(recv_ref, coef_ref, slot_ref, partial_ref, now_ref, last_ref, sums_ref, faces_ref,
              yh, xh, yl, xl, frac_ref, matrix_ref, seen):
    inflow = flow_in(now_ref[...], faces_ref, xl, xh, yl, yh)
    matrix_ref[...] = (last_ref[...] + inflow) * sums_ref[0]
    blocks = partial_ref.shape[0]
    unpack(recv_ref, slot_ref, None, seen, blocks)
    own, left, right, pull = [coef_ref[i] for i in range(4)]
    now = partial_ref[...] + pull * seen[0]
    frac_ref[...] = own + left * shift_right(now) + right * shift_left(now) + pull * seen[1]


def trade(block, axis, first):
    flow, cross = lax.axis_size("flow"), lax.axis_size("cross")
    if flow * cross == 1:
        return block
    step, count = (cross, flow) if axis == "flow" else (1, cross)
    pairs = []
    for i in range(flow * cross):
        at = i // step % count
        to = at + 1 if (at % 2 == 0) == first else at - 1
        other = i ^ (1 if axis == "flow" else cross)
        pairs.append((i, i + (to - at) * step if 0 <= to < count else other))
    return lax.ppermute(block, ("flow", "cross"), pairs)


def swap(faces):
    y_first = trade(faces[2], "cross", True)
    y_second = trade(faces[3], "cross", False)
    x_first = trade(faces[0], "flow", True)
    x_second = trade(faces[1], "flow", False)
    return y_second, x_second, y_first, x_first


def deliver(payload):
    return lax.all_to_all(payload, ("flow", "cross"), split_axis=0, concat_axis=0, tiled=True)


def on_device(
    matrix_start, storage, perm, frac_start, frac_store, frac_cond,
    segment_ids, block_counts, hit_tile, hit_cell, hit_weight,
):
    blocks = frac_start.shape[0]
    nx, ny, nz = matrix_start.shape
    rows = nx * ny
    start, storage, perm = [a.reshape(rows, nz) for a in (matrix_start, storage, perm)]
    field = shape(rows, nz)
    faces_of = lambda n: (shape(n * ny, nz),) * 2 + (shape(n * nx + 8, nz),) * 2
    owned = lambda dtype: pltpu.VMEM((blocks, LANES), dtype)

    hits, coef, slots = call(
        owner_first,
        (shape(512, 128), shape(5, blocks, LANES), shape(2, blocks, LANES, dtype=I32)),
        8,
        scratch=[
            owned(F32), owned(F32), owned(F32), owned(I32),
            pltpu.VMEM((2 * blocks, 128), I32), owned(I32), owned(F32),
            pltpu.SemaphoreType.DMA((7,)),
            pltpu.VMEM((10, blocks, LANES), F32),
        ],
        smem=(0,),
        remote=range(1, 8),
        microseconds=6,
        vmem=64 * 1024 * 1024 - 4096,
    )(
        block_counts, frac_start, frac_store, frac_cond, segment_ids,
        hit_tile.reshape(2 * blocks, 128), hit_cell, hit_weight,
    )
    hits = deliver(hits)
    around = swap(call(rock_faces, faces_of(2), 2)(perm, start))
    sums, cells = call(
        tile_scatter,
        (shape(4, rows, nz), shape(2, PAD_RANKS, LANES, dtype=I32)),
        1,
        scratch=[pltpu.VMEM((8, PAD_RANKS, LANES), F32)],
        microseconds=4,
    )(hits)
    found = pltpu.VMEM((2 * PAD_RANKS, LANES), F32)
    y_side, x_side = shape(4 * nx, nz), shape(4 * ny, nz)
    seen, first, sums, faces, known, x_a, x_b = call(
        tile_first,
        (shape(256, 128), field, shape(3, rows, nz), shape(6, rows, nz), field, x_side, x_side),
        9,
        scratch=[found, pltpu.VMEM((256, 128), F32), pltpu.SemaphoreType.DMA((1,))],
        early=True,
        microseconds=4,
    )(sums, cells, perm, start, storage, *around)
    seen = deliver(seen)
    beside_x = trade(x_b, "flow", False), trade(x_a, "flow", True)

    pushed, partial = call(
        owner_middle,
        (shape(256, 128), shape(blocks, LANES)),
        6,
        remote=(4, 5),
        scratch=[
            pltpu.VMEM((blocks, LANES, LANES), BF16),
            pltpu.VMEM((2, blocks, LANES), F32),
            pltpu.VMEM((4, blocks, LANES), F32),
        ],
        microseconds=5,
    )(seen, frac_start, coef, slots, *beside_x)
    pushed = deliver(pushed)
    second, y_a, y_b = call(tile_second, (field, y_side, y_side), 7, remote=(6,))(
        known, first, sums, faces, *beside_x, partial
    )
    beside_y = trade(y_b, "cross", False), trade(y_a, "cross", True)

    hits = call(
        tile_scatter_again,
        shape(2, rows, nz),
        2,
        scratch=[pltpu.VMEM((4, PAD_RANKS, LANES), F32)],
        microseconds=3,
    )(pushed, cells)
    seen, third, last, *sides = call(
        tile_third,
        (shape(256, 128), field, field) + faces_of(1),
        10,
        scratch=[found, pltpu.VMEM((256, 128), F32), pltpu.SemaphoreType.DMA((1,))],
        early=True,
        microseconds=4,
    )(hits, second, first, sums, faces, cells, *beside_y, *beside_x)
    seen = deliver(seen)
    around = swap(sides)
    frac, fourth = call(
        last_pair,
        (shape(blocks, LANES), field),
        12,
        scratch=[pltpu.VMEM((2, blocks, LANES), F32)],
        microseconds=4,
    )(seen, coef, slots, partial, third, last, sums, faces, *around)
    return fourth.reshape(nx, ny, nz), frac


def solution(mesh):
    grid = P("flow", "cross", None)
    owner = P(("flow", "cross"), None)
    counts, tiles = P(("flow", "cross")), P(("flow", "cross"), None, None)
    in_specs = (grid,) * 3 + (owner,) * 4 + (counts, tiles, owner, owner)
    return jax.shard_map(
        on_device, mesh=mesh, in_specs=in_specs, out_specs=(grid, owner), check_vma=False
    )
```
